512 devices in a mesh: wide: 64 (over y, z), narrow: 4 (over x), chip: 2 (over core).
Axes of the slice: x: 4, y: 4, z: 16, core: 2. Of those that a mesh axis runs over, the one named last changes fastest.
Arguments:
- right_side: float32 [100, 131072], P(None, ('wide', 'narrow', 'chip')), may hold values from -24 to 24
- orders: int32 [131072], P(('wide', 'narrow', 'chip')), may hold values from 4 to 9
- elem_scale: float32 [131072], P(('wide', 'narrow', 'chip')), may hold values from 0.5 to 2
- neighbours: int32 [4, 131072], P(None, ('wide', 'narrow', 'chip')), may hold values from 0 to 767
- rebalance: int32 [131072], P(('wide', 'narrow', 'chip')), may hold values from 0 to 2047, as said below
- mode_diag: float32 [100], replicated, may hold values from 2 to 4
- stiffness: float32 [100, 100], replicated, may hold values from -0.625 to 0.625
- coupling: float32 [100, 100], replicated, may hold values from -0.625 to 0.625
- block_inverse: float32 [6, 100, 100], replicated, may hold values from -0.625 to 0.625
Outputs:
- solution: float32 [100, 131072], P(None, ('wide', 'narrow', 'chip'))
The draws below stay inside these ranges and needn't reach their ends.
Inputs may be any that keep to these rules, and one draw needn't show every extreme that they name: `rebalance`: within each group of 2048 consecutive elements, every group-local index appears exactly once.
All inputs are finite; a program needn't handle non-finite values.
Results may differ from the reference program's by a relative error of at most 0.0003.
Values sent between devices are 32-bit elements; how exact they have to be, the bound alone decides.
A program may use at most 64 MiB of HBM per device.

```python
import math
import jax
import jax.numpy as jnp
from jax import lax

MAX_ORDER = 9
MIN_ORDER = 4
M = 100
NORDERS = 6
E_DEV = 256
SWEEPS = 3
GROUP = 2048
NE = 131072
N_WIDE = 64


def draw_rebalance(key, part):
    key = jax.random.fold_in(key, 7)
    subkeys = jax.random.split(key, N_WIDE)
    perms = jax.vmap(lambda sub_key: jax.random.permutation(sub_key, GROUP))(subkeys)
    return perms.reshape(-1).astype(jnp.int32)


def ramp_scale(ratio):
    position = jnp.arange(NE, dtype=jnp.float32) / jnp.float32(NE)
    return jnp.exp(jnp.log(jnp.float32(ratio)) * position)[None, :]


def draw_right_side(key, part):
    key = jax.random.fold_in(key, 11)
    values = jnp.clip(jax.random.normal(key, (M, NE), jnp.float32), -5.0, 5.0)
    return (values * ramp_scale(4.0)).astype(jnp.float32)


def plant(result, own_key, smallest, high):
    longest = result.shape.index(max(result.shape))
    spots = []
    for shift in (0, 1):
        where = [jax.random.randint(jax.random.fold_in(own_key, axis), (), 0, length) for axis, length in enumerate(result.shape)]
        where[longest] = (where[longest] + shift) % result.shape[longest]
        spots.append(tuple(where))
    return result.at[spots[0]].set(smallest).at[spots[1]].set(high)


def shard_levels(key, shape, cuts, smallest, top_value):
    loudness = 1.0
    for dim, parts in cuts:
        heights = jax.random.uniform(jax.random.fold_in(jax.random.fold_in(key, 6), dim), (parts,), jnp.float32, smallest / len(cuts), top_value / len(cuts))
        loudness = loudness * jnp.repeat(jnp.exp(heights), shape[dim] // parts).reshape((-1,) + (1,) * (len(shape) - 1 - dim))
    return loudness


def scatter_about(key, dims, width, bound, held_as=jnp.bfloat16):
    values = width * jax.random.normal(key, dims, jnp.float32)
    return jnp.clip(values, min=-bound, max=bound).astype(held_as)


def setup_inputs(seed: int = 0) -> dict:
    key_of = jax.random.split(jax.random.key(seed), 10)
    right_side = draw_right_side(jax.random.fold_in(key_of[9], 71), 0)
    orders = plant(jax.random.randint(key_of[1], (NE,), MIN_ORDER, MAX_ORDER + 1), jax.random.fold_in(key_of[1], 1), MIN_ORDER, MAX_ORDER).astype(jnp.int32)
    elem_scale = jnp.clip(jnp.exp(math.log(2.0) - 1.3862944 * jax.random.uniform(key_of[2], (NE,), jnp.float32) ** shard_levels(key_of[2], (NE,), ((0, 512),), -0.2, 0.2)), 0.5, 2.0)
    neighbours = plant(jax.random.randint(key_of[3], (4, NE), 0, 3 * E_DEV), jax.random.fold_in(key_of[3], 1), 0, (3 * E_DEV) - 1).astype(jnp.int32)
    rebalance = draw_rebalance(jax.random.fold_in(key_of[9], 71), 0)
    mode_diag = jnp.clip(jax.random.uniform(key_of[5], (M,), jnp.float32, 2.0, 4.0), 2.0, 4.0)
    stiffness = scatter_about(key_of[6], (M, M), M ** -0.5, 0.625, jnp.float32)
    coupling = scatter_about(key_of[7], (M, M), M ** -0.5, 0.625, jnp.float32)
    block_inverse = scatter_about(key_of[8], (NORDERS, M, M), M ** -0.5, 0.625, jnp.float32)
    return dict(right_side=right_side, orders=orders, elem_scale=elem_scale, neighbours=neighbours, rebalance=rebalance, mode_diag=mode_diag, stiffness=stiffness, coupling=coupling, block_inverse=block_inverse)


SHIFT_SIGMA = 0.5
FACE_WEIGHT = 0.25
PAIR_WEIGHT = 0.5

def coarse_index():
    per_side = MAX_ORDER + 1
    return jnp.array([0, 1, per_side, per_side + 1], dtype=jnp.int32)

def keep_table(orders):
    mode_ids = jnp.arange(M, dtype=jnp.int32)
    row_degree = mode_ids // (MAX_ORDER + 1)
    col_degree = mode_ids % (MAX_ORDER + 1)
    is_kept = (row_degree[:, None] <= orders[None, :]) & (col_degree[:, None] <= orders[None, :])
    return is_kept.astype(jnp.float32)

def matmul(matrix, operand):
    return jnp.dot(matrix, operand, precision=lax.Precision.HIGHEST, preferred_element_type=jnp.float32)

def face_total(vector, neighbours, within_group):
    element_count = vector.shape[1]
    elements = jnp.arange(element_count, dtype=jnp.int32)
    offset = elements // E_DEV * E_DEV - E_DEV
    summed = jnp.zeros(vector.shape, jnp.float32)
    for which_face in range(4):
        target = offset + neighbours[which_face]
        is_valid = (target >= 0) & (target < element_count)
        if within_group:
            is_valid = is_valid & (target // GROUP == elements // GROUP)
        picked = jnp.take(vector, jnp.clip(target, 0, element_count - 1), axis=1)
        summed = summed + jnp.where(is_valid[None, :], picked, jnp.float32(0.0))
    return summed

def operate(vector, elem_scale, mode_diag, stiffness, coupling, neighbours, mode_keep):
    neighbour_sum = face_total(vector, neighbours, False)
    own_part = elem_scale[None, :] * (mode_diag[:, None] * vector + matmul(stiffness, vector))
    return mode_keep * (own_part - SHIFT_SIGMA * vector - FACE_WEIGHT * matmul(coupling, neighbour_sum))

def coarse_solve(coarse_rhs, elem_scale, mode_diag, stiffness, coupling, neighbours):
    coarse_idx = coarse_index()
    diag_c = mode_diag[coarse_idx]
    stiff_c = stiffness[coarse_idx][:, coarse_idx]
    gain_c = coupling[coarse_idx][:, coarse_idx]
    inverse = 1.0 / (elem_scale[None, :] * (diag_c + jnp.diagonal(stiff_c))[:, None] - SHIFT_SIGMA)
    coarse = inverse * coarse_rhs
    for step_index in range(SWEEPS - 1):
        neighbour_sum = face_total(coarse, neighbours, True)
        coarse_image = elem_scale[None, :] * (diag_c[:, None] * coarse + matmul(stiff_c, coarse)) - SHIFT_SIGMA * coarse - FACE_WEIGHT * matmul(gain_c, neighbour_sum)
        coarse = coarse + inverse * (coarse_rhs - coarse_image)
    return coarse

def partner_index(rebalance):
    element_count = rebalance.shape[0]
    slots = jnp.arange(element_count, dtype=jnp.int32)
    group_base = slots // GROUP * GROUP
    holder = group_base + rebalance
    partner = group_base + rebalance[slots ^ 1]
    return jnp.zeros((element_count,), jnp.int32).at[holder].set(partner)

def precondition(vector, orders, mode_keep, partner, elem_scale, neighbours, mode_diag, stiffness, coupling, block_inverse):
    mixed = vector + PAIR_WEIGHT * jnp.take(vector, partner, axis=1)
    smoothed = jnp.zeros(vector.shape, jnp.float32)
    for order_slot in range(NORDERS):
        smoothed = smoothed + jnp.where((orders == order_slot + MIN_ORDER)[None, :], matmul(block_inverse[order_slot], mixed), jnp.float32(0.0))
    coarse_idx = coarse_index()
    coarse = coarse_solve(vector[coarse_idx], elem_scale, mode_diag, stiffness, coupling, neighbours)
    return (mode_keep * smoothed).at[coarse_idx].add(coarse)

def reference(right_side, orders, elem_scale, neighbours, rebalance, mode_diag, stiffness, coupling, block_inverse):
    mode_keep = keep_table(orders)
    partner = partner_index(rebalance)

    def apply_op(vector):
        return operate(vector, elem_scale, mode_diag, stiffness, coupling, neighbours, mode_keep)

    def apply_pre(vector):
        return precondition(vector, orders, mode_keep, partner, elem_scale, neighbours, mode_diag, stiffness, coupling, block_inverse)
    start = mode_keep * right_side
    start_norm = jnp.sqrt(jnp.sum(start * start))
    basis_one = start / start_norm
    dir_one = apply_pre(basis_one)
    image_one = apply_op(dir_one)
    proj_aa = jnp.sum(basis_one * image_one)
    resid_one = image_one - proj_aa * basis_one
    height_one = jnp.sqrt(jnp.sum(resid_one * resid_one))
    basis_two = resid_one / height_one
    dir_two = apply_pre(basis_two)
    image_two = apply_op(dir_two)
    proj_ab = jnp.sum(basis_one * image_two)
    proj_bb = jnp.sum(basis_two * image_two)
    resid_two = image_two - proj_ab * basis_one - proj_bb * basis_two
    height_two = jnp.sqrt(jnp.sum(resid_two * resid_two))
    radius_one = jnp.sqrt(proj_aa * proj_aa + height_one * height_one)
    cos_one = proj_aa / radius_one
    sin_one = height_one / radius_one
    upper_ab = cos_one * proj_ab + sin_one * proj_bb
    lower_bb = cos_one * proj_bb - sin_one * proj_ab
    rhs_first = cos_one * start_norm
    rhs_second = -sin_one * start_norm
    radius_two = jnp.sqrt(lower_bb * lower_bb + height_two * height_two)
    cos_two = lower_bb / radius_two
    coef_two = cos_two * rhs_second / radius_two
    coef_one = (rhs_first - upper_ab * coef_two) / radius_one
    return coef_one * dir_one + coef_two * dir_two
```

```python
import functools

import jax
import jax.numpy as jnp
from jax import lax
from jax.experimental import pallas as pl
from jax.experimental.pallas import tpu as pltpu
from jax.sharding import PartitionSpec as P

M = 100
MT = 104
MP = 112
E = 256
HALF = 56
ORDERS = 6
MIN_ORDER = 4
SHIFT = 0.5
COARSE = (0, 1, 10, 11)
MESH = pl.DeviceIdType.MESH
F32 = jnp.float32
BF16 = jnp.bfloat16


def two_sum(a, b):
    s = a + b
    t = s - a
    return s, (a - (s - t)) + (b - t)


def halves(a):
    t = a * F32(4097.0)
    hi = t - (t - a)
    return hi, a - hi


def two_prod(a, b, a_parts=None, b_parts=None):
    ah, al = halves(a) if a_parts is None else a_parts
    bh, bl = halves(b) if b_parts is None else b_parts
    p = a * b
    return p, ((ah * bh - p) + ah * bl + al * bh) + al * bl


def dd_add(a, b):
    s, e = two_sum(a[0], b[0])
    return two_sum(s, e + (a[1] + b[1]))


def dd_neg(a):
    return -a[0], -a[1]


def dd_mul(a, b):
    p, e = two_prod(a[0], b[0])
    return two_sum(p, e + (a[0] * b[1] + a[1] * b[0]))


def dd_div(a, b):
    q = a[0] / b[0]
    r = dd_add(a, dd_neg(dd_mul((q, jnp.zeros_like(q)), b)))
    return two_sum(q, (r[0] + r[1]) / b[0])


def split(x):
    hi = x.astype(BF16)
    return hi, (x - hi.astype(F32)).astype(BF16)


def dot(a, b):
    return jnp.dot(a, b, preferred_element_type=F32)


def iota(shape, axis):
    return lax.broadcasted_iota(jnp.int32, shape, axis)


def pad_rows(x):
    return jnp.concatenate([x, jnp.zeros((MP - MT, x.shape[1]), F32)], axis=0)


def fold(d):
    return d[:MP] + d[MP:]


def kernel(
    sizes, rs, ords, scale, nb, reb, diag, st, cp, bi, out,
    v, ag, z, halo, rebg, cw, nbg, rsrc, red, pad, cpad, bl, sl, cl, tsel, fsel, gl, wl, mh, ml, kh, kl,
    ag_s, ag_r, reb_s, reb_r, cw_s, cw_r, nb_s, nb_r, halo_s, halo_r, red_s, red_r,
):
    n_wide, n_y, n_z = sizes
    w, x, c = lax.axis_index("wide"), lax.axis_index("narrow"), lax.axis_index("chip")
    p = 2 * x + c
    line = w * 8 + p
    total = n_wide * 8
    wy, wz = w // n_z, w % n_z

    def group_dev(off):
        q = (p + off + 8) % 8
        return (w, q // 2, q % 2)

    def line_dev(off):
        q = (line + off + total) % total
        return (q // 8, (q % 8) // 2, q % 2)

    def y_dev(off):
        return (((wy + off) % n_y) * n_z + wz, x, c)

    def z_dev(off):
        return (wy * n_z + (wz + off) % n_z, x, c)

    right, left = (w, (x + 1) % 4, c), (w, (x + 3) % 4, c)
    sib = (w, x, 1 - c)

    barrier = pltpu.get_barrier_semaphore()
    greeted = (
        [group_dev(o) for o in range(1, 8)]
        + [line_dev(1), line_dev(-1)]
        + [y_dev(o) for o in range(1, n_y)]
        + [z_dev(o) for o in range(1, n_z)]
    )
    for d in greeted:
        pl.semaphore_signal(barrier, inc=1, device_id=d, device_id_type=MESH)

    mode = iota((MT, E), 0)
    row_degree = (mode * 103) >> 10
    degree = jnp.maximum(row_degree, mode - 10 * row_degree)
    kept = jnp.where(degree <= ords[...], F32(1.0), F32(0.0))
    v[0, 96:MT, :] = jnp.zeros((8, E), F32)
    v[0, 0:M, :] = kept[0:M] * rs[...]
    rebg[0:1, :] = reb[...]
    for it in range(2):
        cw[it, 2] = jnp.zeros((8, E), F32)
        cw[it, 2, 4:5, :] = scale[...]

    def coarse_rows(it):
        cw[it, 2, 0:2, :] = v[it, 0:2, :]
        cw[it, 2, 2:4, :] = v[it, 10:12, :]

    coarse_rows(0)
    for stage, count in enumerate((8, n_y, n_z)):
        if count < 16:
            red[stage, count:16, :] = jnp.zeros((16 - count, 128), F32)
    pl.semaphore_wait(barrier, len(greeted))

    def remote(src, dst, ssem, rsem, d):
        return pltpu.make_async_remote_copy(
            src_ref=src, dst_ref=dst, send_sem=ssem, recv_sem=rsem, device_id=d, device_id_type=MESH
        )

    pending = []

    def start(copy):
        copy.start()
        pending.append(copy)
        return copy

    def send_coarse(it):
        copies = []
        for i, o in enumerate((1, -1, 2, -2)):
            copies.append(
                start(remote(cw.at[it, 2], cw.at[it, 2 - o], cw_s.at[it, i], cw_r.at[it, i], group_dev(o)))
            )
        return copies

    parts = (pl.ds(0, HALF), pl.ds(HALF, MT - HALF))

    def send_block(it):
        def ag_copy(i, src, r, k, part, d):
            return start(
                remote(src.at[part], ag.at[it, r, k].at[part], ag_s.at[it, i], ag_r.at[it, i], d)
            )

        own = v.at[it]
        a_right = ag_copy(0, own, 3, 0, parts[0], right)
        b_left = ag_copy(1, own, 1, 0, parts[1], left)
        b_right = ag_copy(2, own, 3, 0, parts[1], right)
        a_left = ag_copy(3, own, 1, 0, parts[0], left)
        to_sib = ag_copy(4, own, 0, 1, pl.ds(0, MT), sib)

        def pass_on(i, r, h):
            return ag_copy(i, ag.at[it, r, 0], r, 1, parts[h], sib)

        def stage_one():
            a_right.wait_recv()
            relay_a = ag_copy(5, ag.at[it, 3, 0], 2, 0, parts[0], right)
            f0 = pass_on(6, 3, 0)
            b_left.wait_recv()
            relay_b = ag_copy(7, ag.at[it, 1, 0], 2, 0, parts[1], left)
            f1 = pass_on(8, 1, 1)
            return relay_a, relay_b, f0, f1

        def stage_two():
            b_right.wait_recv()
            f2 = pass_on(9, 3, 1)
            a_left.wait_recv()
            f3 = pass_on(10, 1, 0)
            return f2, f3

        def stage_three(relay_a, relay_b):
            relay_a.wait_recv()
            f4 = pass_on(11, 2, 0)
            relay_b.wait_recv()
            f5 = pass_on(12, 2, 1)
            return f4, f5

        return to_sib, stage_one, stage_two, stage_three

    blocks = ((0, 0), (0, 1), (3, 0), (1, 0), (3, 1), (1, 1), (2, 0), (2, 1))

    def put_block(it, b):
        r, k = blocks[b]
        value = v[it] if b == 0 else ag[it, r, k]
        hi, lo = split(pad_rows(value))
        gl[0:MP, b * E : (b + 1) * E] = hi
        gl[MP:, b * E : (b + 1) * E] = lo

    def gather(b0, b1):
        return fold(dot(gl[:, b0 * E : b1 * E], tsel[b0 * E : b1 * E, :]))

    def prepare_matrices():
        pad[...] = jnp.zeros(pad.shape, F32)
        for o in range(ORDERS):
            pad[o, 0:M, 0:M] = bi[o]
        pad[6, 0:M, 0:M] = st[...]
        pad[7, 0:M, 0:M] = F32(0.25) * cp[...]
        pad[8, 0:1, 0:M] = diag[...]
        for o in range(ORDERS):
            hi, lo = split(pad[o])
            bl[0:MP, o * 128 : (o + 1) * 128] = hi
            bl[MP:, o * 128 : (o + 1) * 128] = lo
        s = pad[6]
        s = s + jnp.where(iota((MP, 128), 0) == iota((MP, 128), 1), pad[8, 0:1, :], F32(0.0))
        hi, lo = split(s)
        sl[0:MP] = hi
        sl[MP:] = lo
        pad[6] = s
        hi, lo = split(pad[7])
        cl[0:MP] = hi
        cl[MP:] = lo
        cpad[...] = jnp.zeros(cpad.shape, F32)
        for i in range(2):
            cpad[i, 0:2, :] = pad[6 + i, 0:2, :]
            cpad[i, 2:4, :] = pad[6 + i, 10:12, :]
        for ref in (kh, kl):
            ref[MP:128] = jnp.zeros((16, E), BF16)
        for o in range(ORDERS):
            for ref in (mh, ml):
                ref[o * 128 + MP : (o + 1) * 128] = jnp.zeros((16, E), BF16)

    def partner_table():
        rows = rebg[...]
        even = iota((8, E), 1) % 2 == 0
        swapped = jnp.where(even, pltpu.roll(rows, E - 1, 1), pltpu.roll(rows, 1, 1)).astype(F32)
        me = iota((E, 128), 0) + p * E
        acc = jnp.zeros((E, 128), F32)
        for s in range(8):
            for h in range(2):
                lanes = slice(h * 128, (h + 1) * 128)
                acc = acc + jnp.where(rows[s : s + 1, lanes] == me, swapped[s : s + 1, lanes], F32(0.0))
        column = jnp.sum(acc, axis=1, keepdims=True)
        partner = jnp.sum(
            jnp.where(iota((E, E), 0) == iota((E, E), 1), column, F32(0.0)), axis=0, keepdims=True
        ).astype(jnp.int32)
        for b, (r, k) in enumerate(blocks):
            q = 2 * ((x + r) % 4) + (c if k == 0 else 1 - c)
            local = partner - q * E

            @pl.loop(0, E // 64)
            def _(i):
                hit = iota((64, E), 0) + i * 64 == local
                tsel[pl.ds(b * E + i * 64, 64), :] = jnp.where(hit, F32(1.0), F32(0.0)).astype(BF16)

    def face_table(slot, index):
        @pl.loop(0, 3 * E // 64)
        def _(i):
            here = iota((64, E), 0) + i * 64
            count = jnp.zeros((64, E), F32)
            for f in range(4):
                count = count + jnp.where(here == index[f], F32(1.0), F32(0.0))
            fsel[slot, pl.ds(i * 64, 64), :] = count.astype(BF16)

    def coarse_solve(it):
        row = iota((8, E), 0)
        stiff = cpad[0]
        gain = cpad[1]
        s_col = [stiff[:, m : m + 1] for m in COARSE]
        g_col = [gain[:, m : m + 1] for m in COARSE]
        row1 = iota((8, 1), 0)
        dsum = jnp.zeros((8, 1), F32)
        for j in range(4):
            dsum = dsum + jnp.where(row1 == j, s_col[j], F32(0.0))
        rhs, scales, inverse, valid, y = [], [], [], [], []
        for o in range(-2, 3):
            ok = jnp.logical_and(p + o >= 0, p + o < 8)
            block = jnp.where(ok, cw[it, o + 2], F32(0.0))
            rhs.append(jnp.where(row < 4, block, F32(0.0)))
            scales.append(block[4:5])
            inverse.append(F32(1.0) / (block[4:5] * dsum - F32(SHIFT)))
            valid.append(ok)
            y.append(inverse[-1] * rhs[-1])

        def update(i, slot, y):
            window = jnp.concatenate([y[i - 1], y[i], y[i + 1]], axis=1)
            hi = window.astype(BF16).astype(F32)
            both = jnp.concatenate([hi, window - hi], axis=0).astype(BF16)
            d = dot(both, fsel[slot])
            nsum = d[0:8] + d[8:16]
            own = jnp.zeros((8, E), F32)
            faces = jnp.zeros((8, E), F32)
            for j in range(4):
                own = own + s_col[j] * y[i][j : j + 1]
                faces = faces + g_col[j] * nsum[j : j + 1]
            image = scales[i] * own - F32(SHIFT) * y[i] - faces
            new = y[i] + inverse[i] * (rhs[i] - image)
            return jnp.where(valid[i], new, F32(0.0))

        first = [None] + [update(i, i - 1, y) for i in (1, 2, 3)]
        return update(2, 1, first)

    def smooth(mixed):
        for o in range(ORDERS):
            hi, lo = split(jnp.where(ords[...] == o + MIN_ORDER, mixed, F32(0.0)))
            mh[o * 128 : o * 128 + MP] = hi
            ml[o * 128 : o * 128 + MP] = lo
        return fold(dot(bl[...], mh[...])) + dot(bl[0:MP], ml[...])

    def apply_both(it, block, coarse_copies, nb_copies):
        to_sib, stage_one, stage_two, stage_three = block
        if it == 0:
            prepare_matrices()
            for copy in reb_copies:
                copy.wait_recv()
            partner_table()
        relay_a, relay_b, f0, f1 = stage_one()
        if it == 0:
            face_table(1, [nb[f : f + 1, :] for f in range(4)])
        f2, f3 = stage_two()
        if it == 0:
            for copy in nb_copies:
                copy.wait_recv()
            face_table(0, [nbg[0, f : f + 1, :] for f in range(4)])
            face_table(2, [nbg[1, f : f + 1, :] for f in range(4)])
        put_block(it, 0)
        to_sib.wait_recv()
        put_block(it, 1)
        put_block(it, 2)
        put_block(it, 3)
        mine = gather(0, 4)
        for copy in coarse_copies:
            copy.wait_recv()
        coarse = coarse_solve(it)
        f4, f5 = stage_three(relay_a, relay_b)
        f0.wait_recv()
        f2.wait_recv()
        put_block(it, 4)
        f1.wait_recv()
        f3.wait_recv()
        put_block(it, 5)
        put_block(it, 6)
        mine = mine + gather(4, 7)
        f4.wait_recv()
        f5.wait_recv()
        put_block(it, 7)
        mine = mine + gather(7, 8)

        mixed = pad_rows(v[it]) + F32(0.5) * mine
        keep = jnp.where(degree <= ords[...], F32(1.0), F32(0.0))
        z[it] = keep * smooth(mixed)[:MT]
        z[it, 0:2, :] = z[it, 0:2, :] + coarse[0:2]
        z[it, 10:12, :] = z[it, 10:12, :] + coarse[2:4]

        to_next = start(remote(z.at[it], halo.at[it, 0], halo_s.at[it, 0], halo_r.at[it, 0], line_dev(1)))
        to_prev = start(remote(z.at[it], halo.at[it, 1], halo_s.at[it, 1], halo_r.at[it, 1], line_dev(-1)))

        zv = pad_rows(z[it])
        hi, lo = split(zv)
        wl[0:MP, E : 2 * E] = hi
        wl[MP:, E : 2 * E] = lo
        kh[0:MP] = hi
        kl[0:MP] = lo
        own = fold(dot(sl[...], kh[...])) + dot(sl[0:MP], kl[...])
        base = scale[...] * own - F32(SHIFT) * zv
        nsum = fold(dot(wl[:, E : 2 * E], fsel[1, E : 2 * E, :]))
        for side, (copy, ok) in enumerate(((to_next, line > 0), (to_prev, line < total - 1))):
            copy.wait_recv()
            hi, lo = split(pad_rows(jnp.where(ok, halo[it, side], F32(0.0))))
            at = 2 * side * E
            wl[0:MP, at : at + E] = hi
            wl[MP:, at : at + E] = lo
            nsum = nsum + fold(dot(wl[:, at : at + E], fsel[1, at : at + E, :]))
        hi, lo = split(nsum)
        kh[0:MP] = hi
        kl[0:MP] = lo
        faces = fold(dot(cl[...], kh[...])) + dot(cl[0:MP], kl[...])
        v[it + 1] = keep * (base - faces)[:MT]

    def gram(pairs):
        used = sorted({i for pair in pairs for i in pair})
        acc = {}
        for t in range(MT // 8):
            rows = {i: v[i, 8 * t : 8 * t + 8, :] for i in used}
            cut = {i: halves(rows[i]) for i in used}
            for a, b in pairs:
                prod, err = two_prod(rows[a], rows[b], cut[a], cut[b])
                if t == 0:
                    acc[a, b] = prod, err
                else:
                    s, e = two_sum(acc[a, b][0], prod)
                    acc[a, b] = s, acc[a, b][1] + (e + err)
        sums = []
        for pair in pairs:
            hi, lo = acc[pair]
            s, e = two_sum(hi[:, :128], hi[:, 128:])
            hi, lo = s, lo[:, :128] + lo[:, 128:] + e
            sums.append(roll_sum(hi, lo, 0, (4, 2, 1)))
        return sums

    def roll_sum(hi, lo, axis, shifts):
        for shift in shifts:
            s, e = two_sum(hi, pltpu.roll(hi, shift, axis))
            lo = lo + pltpu.roll(lo, shift, axis) + e
            hi = s
        return hi, lo

    reb_copies = [
        start(remote(rebg.at[pl.ds(0, 1)], rebg.at[pl.ds(o, 1)], reb_s.at[o - 1], reb_r.at[o - 1], group_dev(o)))
        for o in range(1, 8)
    ]
    coarse_copies = send_coarse(0)
    nb_copies = [
        start(remote(nb, nbg.at[0], nb_s.at[0], nb_r.at[0], group_dev(1))),
        start(remote(nb, nbg.at[1], nb_s.at[1], nb_r.at[1], group_dev(-1))),
    ]
    block = send_block(0)
    apply_both(0, block, coarse_copies, nb_copies)
    coarse_rows(1)
    coarse_copies = send_coarse(1)
    block = send_block(1)
    early = gram(((0, 0), (0, 1), (1, 1)))
    apply_both(1, block, coarse_copies, [])
    late = gram(((0, 2), (1, 2), (2, 2)))

    row, lane = iota((8, 128), 0), iota((8, 128), 1)
    hi = jnp.zeros((8, 128), F32)
    lo = jnp.zeros((8, 128), F32)
    for i, (h, l) in enumerate(early + late):
        hi = jnp.where(row == i, h, hi)
        lo = jnp.where(row == i, l, lo)
    hi, lo = roll_sum(hi, lo, 1, (64, 32, 16, 8, 4, 2, 1))
    packed = jnp.where(lane == row, hi, F32(0.0)) + jnp.where(lane == row + 8, lo, F32(0.0))
    rsrc[0, 0:1, :] = jnp.sum(packed, axis=0, keepdims=True)

    base = 0
    for stage, (count, target) in enumerate(((8, group_dev), (n_y, y_dev), (n_z, z_dev))):
        copies = []
        for o in range(1, count):
            copies.append(
                start(
                    remote(
                        rsrc.at[stage, pl.ds(0, 1)],
                        red.at[stage, pl.ds(o, 1)],
                        red_s.at[base + o - 1],
                        red_r.at[base + o - 1],
                        target(o),
                    )
                )
            )
        red[stage, 0:1, :] = rsrc[stage, 0:1, :]
        base += count - 1
        for copy in copies:
            copy.wait_recv()
        got = red[stage]
        hi = jnp.where(iota((16, 128), 1) < 8, got, F32(0.0))
        lo = jnp.where(iota((16, 128), 1) < 8, pltpu.roll(got, 120, 1), F32(0.0))
        s, e = two_sum(hi[0:8], hi[8:16])
        hi, lo = s, lo[0:8] + lo[8:16] + e
        hi, lo = roll_sum(hi, lo, 0, (4, 2, 1))
        if stage < 2:
            rsrc[stage + 1, 0:1, :] = (hi + pltpu.roll(lo, 8, 1))[0:1]

    def pick(i):
        h = jnp.sum(jnp.where(lane == i, hi, F32(0.0)), axis=1, keepdims=True)
        l = jnp.sum(jnp.where(lane == i, lo, F32(0.0)), axis=1, keepdims=True)
        return two_sum(h, l)

    g01, g11, g02, g12, g22 = (pick(i) for i in range(1, 6))
    q = dd_div(g12, g11)
    top = dd_add(g02, dd_neg(dd_mul(q, g01)))
    bottom = dd_add(g22, dd_neg(dd_mul(q, g12)))
    beta = (top[0] + top[1]) / (bottom[0] + bottom[1])
    rest = dd_add(g01, dd_neg(dd_mul((beta, jnp.zeros_like(beta)), g12)))
    alpha = (rest[0] + rest[1]) / (g11[0] + g11[1])
    out[...] = alpha[0:1] * z[0, 0:M, :] + beta[0:1] * z[1, 0:M, :]
    for copy in pending:
        copy.wait_send()


def solution(mesh):
    n_wide = mesh.shape["wide"]
    n_z = 16 if n_wide == 64 else n_wide
    n_y = n_wide // n_z

    def per_device(right_side, orders, elem_scale, neighbours, rebalance, mode_diag, stiffness, coupling, block_inverse):
        vmem = pl.BlockSpec(memory_space=pltpu.VMEM)
        dma = pltpu.SemaphoreType.DMA
        return pl.pallas_call(
            functools.partial(kernel, (n_wide, n_y, n_z)),
            out_shape=jax.ShapeDtypeStruct((M, E), F32),
            in_specs=[vmem] * 9,
            out_specs=vmem,
            scratch_shapes=[
                pltpu.VMEM((3, MT, E), F32),
                pltpu.VMEM((2, 4, 2, MT, E), F32),
                pltpu.VMEM((2, MT, E), F32),
                pltpu.VMEM((2, 2, MT, E), F32),
                pltpu.VMEM((8, E), jnp.int32),
                pltpu.VMEM((2, 5, 8, E), F32),
                pltpu.VMEM((2, 4, E), jnp.int32),
                pltpu.VMEM((3, 8, 128), F32),
                pltpu.VMEM((3, 16, 128), F32),
                pltpu.VMEM((9, MP, 128), F32),
                pltpu.VMEM((2, 8, 128), F32),
                pltpu.VMEM((2 * MP, ORDERS * 128), BF16),
                pltpu.VMEM((2 * MP, 128), BF16),
                pltpu.VMEM((2 * MP, 128), BF16),
                pltpu.VMEM((8 * E, E), BF16),
                pltpu.VMEM((3, 3 * E, E), BF16),
                pltpu.VMEM((2 * MP, 8 * E), BF16),
                pltpu.VMEM((2 * MP, 3 * E), BF16),
                pltpu.VMEM((ORDERS * 128, E), BF16),
                pltpu.VMEM((ORDERS * 128, E), BF16),
                pltpu.VMEM((128, E), BF16),
                pltpu.VMEM((128, E), BF16),
                dma((2, 13)),
                dma((2, 13)),
                dma((7,)),
                dma((7,)),
                dma((2, 4)),
                dma((2, 4)),
                dma((2,)),
                dma((2,)),
                dma((2, 2)),
                dma((2, 2)),
                dma((7 + n_y - 1 + n_z - 1,)),
                dma((7 + n_y - 1 + n_z - 1,)),
            ],
            compiler_params=pltpu.CompilerParams(
                collective_id=0, has_side_effects=True, vmem_limit_bytes=48 * 1024 * 1024
            ),
        )(
            right_side,
            orders.reshape(1, E),
            elem_scale.reshape(1, E),
            neighbours,
            rebalance.reshape(1, E),
            mode_diag.reshape(1, M),
            stiffness,
            coupling,
            block_inverse,
        )

    line = ("wide", "narrow", "chip")
    return jax.shard_map(
        per_device,
        mesh=mesh,
        in_specs=(P(None, line), P(line), P(line), P(None, line), P(line), P(), P(), P(), P()),
        out_specs=P(None, line),
        check_vma=False,
    )
```

```python
import functools

import jax
import jax.numpy as jnp
from jax import lax
from jax.experimental import pallas as pl
from jax.experimental.pallas import tpu as pltpu
from jax.sharding import PartitionSpec as P

M = 100
MT = 104
MP = 112
E = 256
ORDERS = 6
MIN_ORDER = 4
SHIFT = 0.5
COARSE = (0, 1, 10, 11)
MESH = pl.DeviceIdType.MESH
F32 = jnp.float32
BF16 = jnp.bfloat16


def two_sum(a, b):
    s = a + b
    t = s - a
    return s, (a - (s - t)) + (b - t)


def halves(a):
    t = a * F32(4097.0)
    hi = t - (t - a)
    return hi, a - hi


def two_prod(a, b, a_parts=None, b_parts=None):
    ah, al = halves(a) if a_parts is None else a_parts
    bh, bl = halves(b) if b_parts is None else b_parts
    p = a * b
    return p, ((ah * bh - p) + ah * bl + al * bh) + al * bl


def dd_add(a, b):
    s, e = two_sum(a[0], b[0])
    return two_sum(s, e + (a[1] + b[1]))


def dd_neg(a):
    return -a[0], -a[1]


def dd_mul(a, b):
    p, e = two_prod(a[0], b[0])
    return two_sum(p, e + (a[0] * b[1] + a[1] * b[0]))


def dd_div(a, b):
    q = a[0] / b[0]
    r = dd_add(a, dd_neg(dd_mul((q, jnp.zeros_like(q)), b)))
    return two_sum(q, (r[0] + r[1]) / b[0])


def split(x):
    hi = x.astype(BF16)
    return hi, (x - hi.astype(F32)).astype(BF16)


def dot(a, b):
    return jnp.dot(a, b, preferred_element_type=F32)


def iota(shape, axis):
    return lax.broadcasted_iota(jnp.int32, shape, axis)


def pad_rows(x):
    return jnp.concatenate([x, jnp.zeros((MP - MT, x.shape[1]), F32)], axis=0)


def fold(d):
    return d[:MP] + d[MP:]


def kernel(
    sizes,
    rs_h, ords_h, scale_h, nb_h, reb_h, diag_h, st_h, cp_h, bi_h, out,
    rs, ords, scale, nb, diag, st, cp, bi,
    v, ag, z, halo, rebg, prow, give, take, cw, nbg, rsrc, red, pad, cpad,
    bl, sl, cl, tsel, fsel, gl, wl, mh, ml, kh, kl,
    in_s, ag_s, ag_r, pr_s, pr_r, give_s, give_r, reb_s, reb_r, cw_s, cw_r, nb_s, nb_r,
    halo_s, halo_r, red_s, red_r, known,
):
    n_wide, n_y, n_z = sizes
    w, x, c = lax.axis_index("wide"), lax.axis_index("narrow"), lax.axis_index("chip")
    p = 2 * x + c
    line = w * 8 + p
    total = n_wide * 8
    wy, wz = w // n_z, w % n_z

    def group_dev(off):
        q = (p + off + 8) % 8
        return (w, q // 2, q % 2)

    def line_dev(off):
        q = (line + off + total) % total
        return (q // 8, (q % 8) // 2, q % 2)

    def plane_dev(off):
        q = (p + off) % 8
        return (((wy + off // 8) % n_y) * n_z + wz, q // 2, q % 2)

    def z_dev(off):
        return (wy * n_z + (wz + off + n_z) % n_z, x, c)

    def both_ways(off):
        return [z_dev(off)] if 2 * off == n_z else [z_dev(off), z_dev(-off)]

    right, left = (w, (x + 1) % 4, c), (w, (x + 3) % 4, c)
    across, sib = (w, (x + 2) % 4, c), (w, x, 1 - c)

    inputs = [
        pltpu.make_async_copy(src, dst, in_s.at[i])
        for i, (src, dst) in enumerate(
            (
                (rs_h, rs), (ords_h, ords), (scale_h, scale), (reb_h, rebg.at[pl.ds(0, 1)]),
                (nb_h, nb), (diag_h, diag), (st_h, st), (cp_h, cp), (bi_h, bi),
            )
        )
    ]
    for copy in inputs[:4]:
        copy.start()

    barrier = pltpu.get_barrier_semaphore()
    columns = [plane_dev(8 * o) for o in range(1, n_y)]
    greeted = [group_dev(o) for o in range(1, 8)] + [line_dev(1), line_dev(-1)] + columns + both_ways(1)
    for d in greeted:
        pl.semaphore_signal(barrier, inc=1, device_id=d, device_id_type=MESH)
    for copy in inputs[4:]:
        copy.start()

    rounds = [columns + both_ways(1)] + [both_ways(o) for o in (2, 4) if 2 * o < n_z]

    def tell(i):
        if i < len(rounds):
            for d in rounds[i]:
                pl.semaphore_signal(known.at[i], inc=1, device_id=d, device_id_type=MESH)

    def hear(i):
        if i < len(rounds):
            pl.semaphore_wait(known.at[i], len(rounds[i]))

    mode = iota((MT, E), 0)
    row_degree = (mode * 103) >> 10
    degree = jnp.maximum(row_degree, mode - 10 * row_degree)
    v[0, 96:MT, :] = jnp.zeros((8, E), F32)
    for copy in inputs[:4]:
        copy.wait()
    kept = jnp.where(degree <= ords[...], F32(1.0), F32(0.0))
    v[0, 0:M, :] = kept[0:M] * rs[...]
    for it in range(2):
        cw[it, 2] = jnp.zeros((8, E), F32)
        cw[it, 2, 4:5, :] = scale[...]

    def coarse_rows(it):
        cw[it, 2, 0:2, :] = v[it, 0:2, :]
        cw[it, 2, 2:4, :] = v[it, 10:12, :]

    coarse_rows(0)
    for stage, count in enumerate((8 * n_y, n_z)):
        if count < 32:
            red[stage, count:32, :] = jnp.zeros((32 - count, 128), F32)
    pl.semaphore_wait(barrier, len(greeted))

    def remote(src, dst, ssem, rsem, d):
        return pltpu.make_async_remote_copy(
            src_ref=src, dst_ref=dst, send_sem=ssem, recv_sem=rsem, device_id=d, device_id_type=MESH
        )

    pending = []

    def start(copy):
        copy.start()
        pending.append(copy)
        return copy

    def send_coarse(it):
        copies = []
        for i, o in enumerate((1, -1, 2, -2)):
            copies.append(
                start(remote(cw.at[it, 2], cw.at[it, 2 - o], cw_s.at[it, i], cw_r.at[it, i], group_dev(o)))
            )
        return copies

    def send_block(it):
        return [
            start(remote(v.at[it], ag.at[it, i], ag_s.at[it, i], ag_r.at[it, i], d))
            for i, d in enumerate((right, left, across))
        ]

    offsets = (0, 3, 1, 2)

    def put_block(it, b):
        hi, lo = split(pad_rows(v[it] if b == 0 else ag[it, b - 1]))
        gl[0:MP, b * E : (b + 1) * E] = hi
        gl[MP:, b * E : (b + 1) * E] = lo

    def gather(b0, b1, half):
        return fold(dot(gl[:, b0 * E : b1 * E], tsel[b0 * E : b1 * E, half * E : (half + 1) * E]))

    def prepare_matrices():
        for copy in inputs[5:]:
            copy.wait()
        pad[...] = jnp.zeros(pad.shape, F32)
        for o in range(ORDERS):
            pad[o, 0:M, 0:M] = bi[o]
        pad[6, 0:M, 0:M] = st[...]
        pad[7, 0:M, 0:M] = F32(0.25) * cp[...]
        pad[8, 0:1, 0:M] = diag[...]
        for o in range(ORDERS):
            hi, lo = split(pad[o])
            bl[0:MP, o * 128 : (o + 1) * 128] = hi
            bl[MP:, o * 128 : (o + 1) * 128] = lo
        s = pad[6]
        s = s + jnp.where(iota((MP, 128), 0) == iota((MP, 128), 1), pad[8, 0:1, :], F32(0.0))
        hi, lo = split(s)
        sl[0:MP] = hi
        sl[MP:] = lo
        pad[6] = s
        hi, lo = split(pad[7])
        cl[0:MP] = hi
        cl[MP:] = lo
        cpad[...] = jnp.zeros(cpad.shape, F32)
        for i in range(2):
            cpad[i, 0:2, :] = pad[6 + i, 0:2, :]
            cpad[i, 2:4, :] = pad[6 + i, 10:12, :]
        for ref in (kh, kl):
            ref[MP:128] = jnp.zeros((16, E), BF16)
        for o in range(ORDERS):
            for ref in (mh, ml):
                ref[o * 128 + MP : (o + 1) * 128] = jnp.zeros((16, E), BF16)

    def partner_table():
        rows = rebg[...]
        even = iota((8, E), 1) % 2 == 0
        swapped = jnp.where(even, pltpu.roll(rows, E - 1, 1), pltpu.roll(rows, 1, 1)).astype(F32)
        me = iota((E, 128), 0) + p * E
        acc = jnp.zeros((E, 128), F32)
        for s in range(8):
            for h in range(2):
                lanes = slice(h * 128, (h + 1) * 128)
                acc = acc + jnp.where(rows[s : s + 1, lanes] == me, swapped[s : s + 1, lanes], F32(0.0))
        column = jnp.sum(acc, axis=1, keepdims=True)
        partner = jnp.sum(
            jnp.where(iota((E, E), 0) == iota((E, E), 1), column, F32(0.0)), axis=0, keepdims=True
        ).astype(jnp.int32)
        prow[0:1, :] = partner
        swap = start(remote(prow.at[pl.ds(0, 1)], prow.at[pl.ds(1, 1)], pr_s, pr_r, sib))
        for half in range(2):
            if half == 1:
                swap.wait_recv()
            for b, r in enumerate(offsets):
                local = prow[half : half + 1, :] - (2 * ((x + r) % 4) + c) * E

                @pl.loop(0, E // 64)
                def _(i):
                    hit = iota((64, E), 0) + i * 64 == local
                    tsel[pl.ds(b * E + i * 64, 64), half * E : (half + 1) * E] = jnp.where(
                        hit, F32(1.0), F32(0.0)
                    ).astype(BF16)

    def face_table(slot, index):
        @pl.loop(0, 3 * E // 64)
        def _(i):
            here = iota((64, E), 0) + i * 64
            count = jnp.zeros((64, E), F32)
            for f in range(4):
                count = count + jnp.where(here == index[f], F32(1.0), F32(0.0))
            fsel[slot, pl.ds(i * 64, 64), :] = count.astype(BF16)

    def coarse_solve(it):
        row = iota((8, E), 0)
        stiff = cpad[0]
        gain = cpad[1]
        s_col = [stiff[:, m : m + 1] for m in COARSE]
        g_col = [gain[:, m : m + 1] for m in COARSE]
        row1 = iota((8, 1), 0)
        dsum = jnp.zeros((8, 1), F32)
        for j in range(4):
            dsum = dsum + jnp.where(row1 == j, s_col[j], F32(0.0))
        rhs, scales, inverse, valid, y = [], [], [], [], []
        for o in range(-2, 3):
            ok = jnp.logical_and(p + o >= 0, p + o < 8)
            block = jnp.where(ok, cw[it, o + 2], F32(0.0))
            rhs.append(jnp.where(row < 4, block, F32(0.0)))
            scales.append(block[4:5])
            inverse.append(F32(1.0) / (block[4:5] * dsum - F32(SHIFT)))
            valid.append(ok)
            y.append(inverse[-1] * rhs[-1])

        def update(i, slot, y):
            window = jnp.concatenate([y[i - 1], y[i], y[i + 1]], axis=1)
            hi = window.astype(BF16).astype(F32)
            both = jnp.concatenate([hi, window - hi], axis=0).astype(BF16)
            d = dot(both, fsel[slot])
            nsum = d[0:8] + d[8:16]
            own = jnp.zeros((8, E), F32)
            faces = jnp.zeros((8, E), F32)
            for j in range(4):
                own = own + s_col[j] * y[i][j : j + 1]
                faces = faces + g_col[j] * nsum[j : j + 1]
            image = scales[i] * own - F32(SHIFT) * y[i] - faces
            new = y[i] + inverse[i] * (rhs[i] - image)
            return jnp.where(valid[i], new, F32(0.0))

        first = [None] + [update(i, i - 1, y) for i in (1, 2, 3)]
        return update(2, 1, first)

    def smooth(mixed):
        for o in range(ORDERS):
            hi, lo = split(jnp.where(ords[...] == o + MIN_ORDER, mixed, F32(0.0)))
            mh[o * 128 : o * 128 + MP] = hi
            ml[o * 128 : o * 128 + MP] = lo
        return fold(dot(bl[...], mh[...])) + dot(bl[0:MP], ml[...])

    def apply_both(it, block, coarse_copies, nb_copies):
        if it == 0:
            for copy in reb_copies:
                copy.wait_recv()
            partner_table()
            prepare_matrices()
            face_table(1, [nb[f : f + 1, :] for f in range(4)])
            for copy in nb_copies:
                copy.wait_recv()
            face_table(0, [nbg[0, f : f + 1, :] for f in range(4)])
            face_table(2, [nbg[1, f : f + 1, :] for f in range(4)])
        put_block(it, 0)
        block[0].wait_recv()
        put_block(it, 1)
        block[1].wait_recv()
        put_block(it, 2)
        theirs = gather(0, 3, 1)
        block[2].wait_recv()
        put_block(it, 3)
        theirs = theirs + gather(3, 4, 1)
        give[it] = theirs[:MT]
        handed = start(remote(give.at[it], take.at[it], give_s.at[it], give_r.at[it], sib))
        mine = gather(0, 4, 0)
        for copy in coarse_copies:
            copy.wait_recv()
        coarse = coarse_solve(it)
        handed.wait_recv()
        mixed = pad_rows(v[it] + F32(0.5) * (mine[:MT] + take[it]))
        keep = jnp.where(degree <= ords[...], F32(1.0), F32(0.0))
        z[it] = keep * smooth(mixed)[:MT]
        z[it, 0:2, :] = z[it, 0:2, :] + coarse[0:2]
        z[it, 10:12, :] = z[it, 10:12, :] + coarse[2:4]

        to_next = start(remote(z.at[it], halo.at[it, 0], halo_s.at[it, 0], halo_r.at[it, 0], line_dev(1)))
        to_prev = start(remote(z.at[it], halo.at[it, 1], halo_s.at[it, 1], halo_r.at[it, 1], line_dev(-1)))

        hear(it)
        tell(it + 1)
        zv = pad_rows(z[it])
        hi, lo = split(zv)
        wl[0:MP, E : 2 * E] = hi
        wl[MP:, E : 2 * E] = lo
        kh[0:MP] = hi
        kl[0:MP] = lo
        own = fold(dot(sl[...], kh[...])) + dot(sl[0:MP], kl[...])
        base = scale[...] * own - F32(SHIFT) * zv
        nsum = fold(dot(wl[:, E : 2 * E], fsel[1, E : 2 * E, :]))
        for side, (copy, ok) in enumerate(((to_next, line > 0), (to_prev, line < total - 1))):
            copy.wait_recv()
            hi, lo = split(pad_rows(jnp.where(ok, halo[it, side], F32(0.0))))
            at = 2 * side * E
            wl[0:MP, at : at + E] = hi
            wl[MP:, at : at + E] = lo
            nsum = nsum + fold(dot(wl[:, at : at + E], fsel[1, at : at + E, :]))
        hi, lo = split(nsum)
        kh[0:MP] = hi
        kl[0:MP] = lo
        faces = fold(dot(cl[...], kh[...])) + dot(cl[0:MP], kl[...])
        v[it + 1] = keep * (base - faces)[:MT]

    def gram(pairs):
        used = sorted({i for pair in pairs for i in pair})
        acc = {}
        for t in range(MT // 8):
            rows = {i: v[i, 8 * t : 8 * t + 8, :] for i in used}
            cut = {i: halves(rows[i]) for i in used}
            for a, b in pairs:
                prod, err = two_prod(rows[a], rows[b], cut[a], cut[b])
                if t == 0:
                    acc[a, b] = prod, err
                else:
                    s, e = two_sum(acc[a, b][0], prod)
                    acc[a, b] = s, acc[a, b][1] + (e + err)
        sums = []
        for pair in pairs:
            hi, lo = acc[pair]
            s, e = two_sum(hi[:, :128], hi[:, 128:])
            hi, lo = s, lo[:, :128] + lo[:, 128:] + e
            sums.append(roll_sum(hi, lo, 0, (4, 2, 1)))
        return sums

    def roll_sum(hi, lo, axis, shifts):
        for shift in shifts:
            s, e = two_sum(hi, pltpu.roll(hi, shift, axis))
            lo = lo + pltpu.roll(lo, shift, axis) + e
            hi = s
        return hi, lo

    reb_copies = [
        start(remote(rebg.at[pl.ds(0, 1)], rebg.at[pl.ds(o, 1)], reb_s.at[o - 1], reb_r.at[o - 1], group_dev(o)))
        for o in range(1, 8)
    ]
    block = send_block(0)
    coarse_copies = send_coarse(0)
    inputs[4].wait()
    nb_copies = [
        start(remote(nb, nbg.at[0], nb_s.at[0], nb_r.at[0], group_dev(1))),
        start(remote(nb, nbg.at[1], nb_s.at[1], nb_r.at[1], group_dev(-1))),
    ]
    tell(0)
    apply_both(0, block, coarse_copies, nb_copies)
    coarse_rows(1)
    block = send_block(1)
    coarse_copies = send_coarse(1)
    early = gram(((0, 0), (0, 1), (1, 1)))
    apply_both(1, block, coarse_copies, [])
    late = gram(((0, 2), (1, 2), (2, 2)))

    row, lane = iota((8, 128), 0), iota((8, 128), 1)

    def tree(x):
        err = None
        while x.shape[0] > 8:
            n = x.shape[0] // 2
            x, e = two_sum(x[:n], x[n:])
            err = e if err is None else err[:n] + err[n:] + e
        for shift in (4, 2, 1):
            x, e = two_sum(x, pltpu.roll(x, shift, 0))
            err = e if err is None else err + pltpu.roll(err, shift, 0) + e
        return x, err

    def carry(x, err):
        at = iota(x.shape, 1)
        return x + pltpu.roll(jnp.where(at < 8, err, F32(0.0)), 8, 1)

    hi = jnp.zeros((8, 128), F32)
    lo = jnp.zeros((8, 128), F32)
    for i, (h, l) in enumerate(early + late):
        hi = jnp.where(row == i, h, hi)
        lo = jnp.where(row == i, l, lo)
    rest = jnp.zeros((112, 128), F32)
    total_row = carry(*tree(jnp.concatenate([hi, lo, rest], axis=0).T))

    hear(2)
    base = 0
    for stage, (count, target) in enumerate(((8 * n_y, plane_dev), (n_z, z_dev))):
        rsrc[stage, 0:1, :] = total_row[0:1]
        copies = []
        for o in range(1, count):
            copies.append(
                start(
                    remote(
                        rsrc.at[stage, pl.ds(0, 1)],
                        red.at[stage, pl.ds(o, 1)],
                        red_s.at[base + o - 1],
                        red_r.at[base + o - 1],
                        target(o),
                    )
                )
            )
        red[stage, 0:1, :] = total_row[0:1]
        base += count - 1
        for copy in copies:
            copy.wait_recv()
        total_row = carry(*tree(red[stage]))

    def pick(i):
        return two_sum(total_row[:, i : i + 1], total_row[:, i + 8 : i + 9])

    g01, g11, g02, g12, g22 = (pick(i) for i in range(1, 6))
    q = dd_div(g12, g11)
    top = dd_add(g02, dd_neg(dd_mul(q, g01)))
    bottom = dd_add(g22, dd_neg(dd_mul(q, g12)))
    beta = (top[0] + top[1]) / (bottom[0] + bottom[1])
    rest = dd_add(g01, dd_neg(dd_mul((beta, jnp.zeros_like(beta)), g12)))
    alpha = (rest[0] + rest[1]) / (g11[0] + g11[1])
    out[...] = alpha[0:1] * z[0, 0:M, :] + beta[0:1] * z[1, 0:M, :]
    for copy in pending:
        copy.wait_send()


def solution(mesh):
    n_wide = mesh.shape["wide"]
    n_z = 16 if n_wide == 64 else n_wide
    n_y = n_wide // n_z

    def per_device(right_side, orders, elem_scale, neighbours, rebalance, mode_diag, stiffness, coupling, block_inverse):
        hbm = pl.BlockSpec(memory_space=pltpu.HBM)
        dma = pltpu.SemaphoreType.DMA
        n_red = 8 * n_y - 1 + n_z - 1
        return pl.pallas_call(
            functools.partial(kernel, (n_wide, n_y, n_z)),
            out_shape=jax.ShapeDtypeStruct((M, E), F32),
            in_specs=[hbm] * 9,
            out_specs=pl.BlockSpec(memory_space=pltpu.VMEM),
            scratch_shapes=[
                pltpu.VMEM((M, E), F32),
                pltpu.VMEM((1, E), jnp.int32),
                pltpu.VMEM((1, E), F32),
                pltpu.VMEM((4, E), jnp.int32),
                pltpu.VMEM((1, M), F32),
                pltpu.VMEM((M, M), F32),
                pltpu.VMEM((M, M), F32),
                pltpu.VMEM((ORDERS, M, M), F32),
                pltpu.VMEM((3, MT, E), F32),
                pltpu.VMEM((2, 3, MT, E), F32),
                pltpu.VMEM((2, MT, E), F32),
                pltpu.VMEM((2, 2, MT, E), F32),
                pltpu.VMEM((8, E), jnp.int32),
                pltpu.VMEM((8, E), jnp.int32),
                pltpu.VMEM((2, MT, E), F32),
                pltpu.VMEM((2, MT, E), F32),
                pltpu.VMEM((2, 5, 8, E), F32),
                pltpu.VMEM((2, 4, E), jnp.int32),
                pltpu.VMEM((2, 8, 128), F32),
                pltpu.VMEM((2, 32, 128), F32),
                pltpu.VMEM((9, MP, 128), F32),
                pltpu.VMEM((2, 8, 128), F32),
                pltpu.VMEM((2 * MP, ORDERS * 128), BF16),
                pltpu.VMEM((2 * MP, 128), BF16),
                pltpu.VMEM((2 * MP, 128), BF16),
                pltpu.VMEM((4 * E, 2 * E), BF16),
                pltpu.VMEM((3, 3 * E, E), BF16),
                pltpu.VMEM((2 * MP, 4 * E), BF16),
                pltpu.VMEM((2 * MP, 3 * E), BF16),
                pltpu.VMEM((ORDERS * 128, E), BF16),
                pltpu.VMEM((ORDERS * 128, E), BF16),
                pltpu.VMEM((128, E), BF16),
                pltpu.VMEM((128, E), BF16),
                dma((9,)),
                dma((2, 3)),
                dma((2, 3)),
                dma,
                dma,
                dma((2,)),
                dma((2,)),
                dma((7,)),
                dma((7,)),
                dma((2, 4)),
                dma((2, 4)),
                dma((2,)),
                dma((2,)),
                dma((2, 2)),
                dma((2, 2)),
                dma((n_red,)),
                dma((n_red,)),
                pltpu.SemaphoreType.REGULAR((3,)),
            ],
            compiler_params=pltpu.CompilerParams(
                collective_id=0, has_side_effects=True, vmem_limit_bytes=60 * 1024 * 1024
            ),
        )(
            right_side,
            orders.reshape(1, E),
            elem_scale.reshape(1, E),
            neighbours,
            rebalance.reshape(1, E),
            mode_diag.reshape(1, M),
            stiffness,
            coupling,
            block_inverse,
        )

    line = ("wide", "narrow", "chip")
    return jax.shard_map(
        per_device,
        mesh=mesh,
        in_specs=(P(None, line), P(line), P(line), P(None, line), P(line), P(), P(), P(), P()),
        out_specs=P(None, line),
        check_vma=False,
    )
```

```python
import functools

import jax
import jax.numpy as jnp
from jax import lax
from jax.experimental import pallas as pl
from jax.experimental.pallas import tpu as pltpu
from jax.sharding import PartitionSpec as P

M = 100
MT = 104
MP = 112
E = 256
ORDERS = 6
MIN_ORDER = 4
SHIFT = 0.5
COARSE = (0, 1, 10, 11)
MESH = pl.DeviceIdType.MESH
F32 = jnp.float32
BF16 = jnp.bfloat16


def two_sum(a, b):
    s = a + b
    t = s - a
    return s, (a - (s - t)) + (b - t)


def halves(a):
    t = a * F32(4097.0)
    hi = t - (t - a)
    return hi, a - hi


def two_prod(a, b, a_parts=None, b_parts=None):
    ah, al = halves(a) if a_parts is None else a_parts
    bh, bl = halves(b) if b_parts is None else b_parts
    p = a * b
    return p, ((ah * bh - p) + ah * bl + al * bh) + al * bl


def dd_add(a, b):
    s, e = two_sum(a[0], b[0])
    return two_sum(s, e + (a[1] + b[1]))


def dd_neg(a):
    return -a[0], -a[1]


def dd_mul(a, b):
    p, e = two_prod(a[0], b[0])
    return two_sum(p, e + (a[0] * b[1] + a[1] * b[0]))


def dd_div(a, b):
    q = a[0] / b[0]
    r = dd_add(a, dd_neg(dd_mul((q, jnp.zeros_like(q)), b)))
    return two_sum(q, (r[0] + r[1]) / b[0])


def split(x):
    hi = x.astype(BF16)
    return hi, (x - hi.astype(F32)).astype(BF16)


def dot(a, b):
    return jnp.dot(a, b, preferred_element_type=F32)


def iota(shape, axis):
    return lax.broadcasted_iota(jnp.int32, shape, axis)


def pad_rows(x):
    return jnp.concatenate([x, jnp.zeros((MP - MT, x.shape[1]), F32)], axis=0)


def fold(d):
    return d[:MP] + d[MP:]


def kernel(
    sizes,
    rs_h, ords_h, scale_h, nb_h, reb_h, diag_h, st_h, cp_h, bi_h, out,
    rs, ords, scale, nb, diag, st, cp, bi,
    v, ag, z, halo, rebg, prow, give, take, cw, nbg, rsrc, red, pad, cpad,
    bl, sl, cl, tsel, fsel, gl, wl, mh, ml, kh, kl,
    in_s, ag_s, ag_r, pr_s, pr_r, give_s, give_r, reb_s, reb_r, cw_s, cw_r, nb_s, nb_r,
    halo_s, halo_r, red_s, red_r, known,
):
    n_wide, n_y, n_z = sizes
    w, x, c = lax.axis_index("wide"), lax.axis_index("narrow"), lax.axis_index("chip")
    p = 2 * x + c
    line = w * 8 + p
    total = n_wide * 8
    wy, wz = w // n_z, w % n_z

    def group_dev(off):
        q = (p + off + 8) % 8
        return (w, q // 2, q % 2)

    def line_dev(off):
        q = (line + off + total) % total
        return (q // 8, (q % 8) // 2, q % 2)

    def plane_dev(off):
        q = (p + off) % 8
        return (((wy + off // 8) % n_y) * n_z + wz, q // 2, q % 2)

    def z_dev(off):
        return (wy * n_z + (wz + off + n_z) % n_z, x, c)

    def both_ways(off):
        return [z_dev(off)] if 2 * off == n_z else [z_dev(off), z_dev(-off)]

    right, left = (w, (x + 1) % 4, c), (w, (x + 3) % 4, c)
    across, sib = (w, (x + 2) % 4, c), (w, x, 1 - c)

    inputs = [
        pltpu.make_async_copy(src, dst, in_s.at[i])
        for i, (src, dst) in enumerate(
            (
                (rs_h, rs), (ords_h, ords), (scale_h, scale), (reb_h, rebg.at[pl.ds(0, 1)]),
                (nb_h, nb), (diag_h, diag), (st_h, st), (cp_h, cp), (bi_h, bi),
            )
        )
    ]
    for copy in inputs[:4]:
        copy.start()

    barrier = pltpu.get_barrier_semaphore()
    near = (4, 3, 5, 2, 6, 1, 7)
    columns = [plane_dev(8 * o) for o in sorted(range(1, n_y), key=lambda o: -min(o, n_y - o))]
    greeted = columns + [line_dev(1), line_dev(-1)] + [group_dev(o) for o in near] + both_ways(1)
    for d in greeted:
        pl.semaphore_signal(barrier, inc=1, device_id=d, device_id_type=MESH)
    for copy in inputs[4:]:
        copy.start()

    rounds = [columns + both_ways(1)] + [both_ways(o) for o in (2, 4) if 2 * o < n_z]

    def tell(i):
        if i < len(rounds):
            for d in rounds[i]:
                pl.semaphore_signal(known.at[i], inc=1, device_id=d, device_id_type=MESH)

    def hear(i):
        if i < len(rounds):
            pl.semaphore_wait(known.at[i], len(rounds[i]))

    mode = iota((MT, E), 0)
    row_degree = (mode * 103) >> 10
    degree = jnp.maximum(row_degree, mode - 10 * row_degree)
    v[0, 96:MT, :] = jnp.zeros((8, E), F32)
    for copy in inputs[:4]:
        copy.wait()
    kept = jnp.where(degree <= ords[...], F32(1.0), F32(0.0))
    v[0, 0:M, :] = kept[0:M] * rs[...]
    for it in range(2):
        cw[it, 2] = jnp.zeros((8, E), F32)
        cw[it, 2, 4:5, :] = scale[...]

    def coarse_rows(it):
        cw[it, 2, 0:2, :] = v[it, 0:2, :]
        cw[it, 2, 2:4, :] = v[it, 10:12, :]

    coarse_rows(0)
    for stage, count in enumerate((8 * n_y, n_z)):
        if count < 32:
            red[stage, count:32, :] = jnp.zeros((32 - count, 128), F32)
    pl.semaphore_wait(barrier, len(greeted))

    def remote(src, dst, ssem, rsem, d):
        return pltpu.make_async_remote_copy(
            src_ref=src, dst_ref=dst, send_sem=ssem, recv_sem=rsem, device_id=d, device_id_type=MESH
        )

    pending = []

    def start(copy):
        copy.start()
        pending.append(copy)
        return copy

    def send_coarse(it):
        copies = []
        for i, o in enumerate((1, -1, 2, -2)):
            copies.append(
                start(remote(cw.at[it, 2], cw.at[it, 2 - o], cw_s.at[it, i], cw_r.at[it, i], group_dev(o)))
            )
        return copies

    def send_block(it):
        copies = [
            start(remote(v.at[it], ag.at[it, i], ag_s.at[it, i], ag_r.at[it, i], d))
            for i, d in ((0, right), (1, left), (2, across))
        ]
        return copies

    offsets = (0, 3, 1, 2)

    def put_block(it, b):
        hi, lo = split(pad_rows(v[it] if b == 0 else ag[it, b - 1]))
        gl[0:MP, b * E : (b + 1) * E] = hi
        gl[MP:, b * E : (b + 1) * E] = lo

    def gather(b0, b1, half):
        return fold(dot(gl[:, b0 * E : b1 * E], tsel[b0 * E : b1 * E, half * E : (half + 1) * E]))

    def prepare_matrices():
        for copy in inputs[5:]:
            copy.wait()
        pad[...] = jnp.zeros(pad.shape, F32)
        for o in range(ORDERS):
            pad[o, 0:M, 0:M] = bi[o]
        pad[6, 0:M, 0:M] = st[...]
        pad[7, 0:M, 0:M] = F32(0.25) * cp[...]
        pad[8, 0:1, 0:M] = diag[...]
        for o in range(ORDERS):
            hi, lo = split(pad[o])
            bl[0:MP, o * 128 : (o + 1) * 128] = hi
            bl[MP:, o * 128 : (o + 1) * 128] = lo
        s = pad[6]
        s = s + jnp.where(iota((MP, 128), 0) == iota((MP, 128), 1), pad[8, 0:1, :], F32(0.0))
        hi, lo = split(s)
        sl[0:MP] = hi
        sl[MP:] = lo
        pad[6] = s
        hi, lo = split(pad[7])
        cl[0:MP] = hi
        cl[MP:] = lo
        cpad[...] = jnp.zeros(cpad.shape, F32)
        for i in range(2):
            cpad[i, 0:2, :] = pad[6 + i, 0:2, :]
            cpad[i, 2:4, :] = pad[6 + i, 10:12, :]
        for ref in (kh, kl):
            ref[MP:128] = jnp.zeros((16, E), BF16)
        for o in range(ORDERS):
            for ref in (mh, ml):
                ref[o * 128 + MP : (o + 1) * 128] = jnp.zeros((16, E), BF16)

    def partner_table():
        rows = rebg[...]
        even = iota((8, E), 1) % 2 == 0
        swapped = jnp.where(even, pltpu.roll(rows, E - 1, 1), pltpu.roll(rows, 1, 1)).astype(F32)
        me = iota((E, 128), 0) + p * E
        acc = jnp.zeros((E, 128), F32)
        for s in range(8):
            for h in range(2):
                lanes = slice(h * 128, (h + 1) * 128)
                acc = acc + jnp.where(rows[s : s + 1, lanes] == me, swapped[s : s + 1, lanes], F32(0.0))
        column = jnp.sum(acc, axis=1, keepdims=True)
        partner = jnp.sum(
            jnp.where(iota((E, E), 0) == iota((E, E), 1), column, F32(0.0)), axis=0, keepdims=True
        ).astype(jnp.int32)
        prow[0:1, :] = partner
        swap = start(remote(prow.at[pl.ds(0, 1)], prow.at[pl.ds(1, 1)], pr_s, pr_r, sib))
        for half in range(2):
            if half == 1:
                swap.wait_recv()
            for b, r in enumerate(offsets):
                local = prow[half : half + 1, :] - (2 * ((x + r) % 4) + c) * E

                @pl.loop(0, E // 64)
                def _(i):
                    hit = iota((64, E), 0) + i * 64 == local
                    tsel[pl.ds(b * E + i * 64, 64), half * E : (half + 1) * E] = jnp.where(
                        hit, F32(1.0), F32(0.0)
                    ).astype(BF16)

    def face_table(slot, index):
        @pl.loop(0, 3 * E // 64)
        def _(i):
            here = iota((64, E), 0) + i * 64
            count = jnp.zeros((64, E), F32)
            for f in range(4):
                count = count + jnp.where(here == index[f], F32(1.0), F32(0.0))
            fsel[slot, pl.ds(i * 64, 64), :] = count.astype(BF16)

    def coarse_solve(it):
        row = iota((8, E), 0)
        stiff = cpad[0]
        gain = cpad[1]
        s_col = [stiff[:, m : m + 1] for m in COARSE]
        g_col = [gain[:, m : m + 1] for m in COARSE]
        row1 = iota((8, 1), 0)
        dsum = jnp.zeros((8, 1), F32)
        for j in range(4):
            dsum = dsum + jnp.where(row1 == j, s_col[j], F32(0.0))
        rhs, scales, inverse, valid, y = [], [], [], [], []
        for o in range(-2, 3):
            ok = jnp.logical_and(p + o >= 0, p + o < 8)
            block = jnp.where(ok, cw[it, o + 2], F32(0.0))
            rhs.append(jnp.where(row < 4, block, F32(0.0)))
            scales.append(block[4:5])
            inverse.append(F32(1.0) / (block[4:5] * dsum - F32(SHIFT)))
            valid.append(ok)
            y.append(inverse[-1] * rhs[-1])

        def update(i, slot, y):
            window = jnp.concatenate([y[i - 1], y[i], y[i + 1]], axis=1)
            hi = window.astype(BF16).astype(F32)
            both = jnp.concatenate([hi, window - hi], axis=0).astype(BF16)
            d = dot(both, fsel[slot])
            nsum = d[0:8] + d[8:16]
            own = jnp.zeros((8, E), F32)
            faces = jnp.zeros((8, E), F32)
            for j in range(4):
                own = own + s_col[j] * y[i][j : j + 1]
                faces = faces + g_col[j] * nsum[j : j + 1]
            image = scales[i] * own - F32(SHIFT) * y[i] - faces
            new = y[i] + inverse[i] * (rhs[i] - image)
            return jnp.where(valid[i], new, F32(0.0))

        first = [None] + [update(i, i - 1, y) for i in (1, 2, 3)]
        return update(2, 1, first)

    def smooth(mixed):
        for o in range(ORDERS):
            hi, lo = split(jnp.where(ords[...] == o + MIN_ORDER, mixed, F32(0.0)))
            mh[o * 128 : o * 128 + MP] = hi
            ml[o * 128 : o * 128 + MP] = lo
        return fold(dot(bl[...], mh[...])) + dot(bl[0:MP], ml[...])

    def apply_both(it, block, coarse_copies, nb_copies):
        if it == 0:
            for copy in reb_copies:
                copy.wait_recv()
            partner_table()
            prepare_matrices()
            face_table(1, [nb[f : f + 1, :] for f in range(4)])
            for copy in nb_copies:
                copy.wait_recv()
            face_table(0, [nbg[0, f : f + 1, :] for f in range(4)])
            face_table(2, [nbg[1, f : f + 1, :] for f in range(4)])
        put_block(it, 0)
        for copy in coarse_copies:
            copy.wait_recv()
        coarse = coarse_solve(it)
        block[0].wait_recv()
        put_block(it, 1)
        block[1].wait_recv()
        put_block(it, 2)
        theirs = gather(0, 3, 1)
        block[2].wait_recv()
        put_block(it, 3)
        theirs = theirs + gather(3, 4, 1)
        give[it] = theirs[:MT]
        handed = start(remote(give.at[it], take.at[it], give_s.at[it], give_r.at[it], sib))
        mine = gather(0, 4, 0)
        handed.wait_recv()
        mixed = pad_rows(v[it] + F32(0.5) * (mine[:MT] + take[it]))
        keep = jnp.where(degree <= ords[...], F32(1.0), F32(0.0))
        z[it] = keep * smooth(mixed)[:MT]
        z[it, 0:2, :] = z[it, 0:2, :] + coarse[0:2]
        z[it, 10:12, :] = z[it, 10:12, :] + coarse[2:4]

        to_next = start(remote(z.at[it], halo.at[it, 0], halo_s.at[it, 0], halo_r.at[it, 0], line_dev(1)))
        to_prev = start(remote(z.at[it], halo.at[it, 1], halo_s.at[it, 1], halo_r.at[it, 1], line_dev(-1)))

        hear(it)
        tell(it + 1)
        zv = pad_rows(z[it])
        hi, lo = split(zv)
        wl[0:MP, E : 2 * E] = hi
        wl[MP:, E : 2 * E] = lo
        kh[0:MP] = hi
        kl[0:MP] = lo
        own = fold(dot(sl[...], kh[...])) + dot(sl[0:MP], kl[...])
        base = scale[...] * own - F32(SHIFT) * zv
        nsum = fold(dot(wl[:, E : 2 * E], fsel[1, E : 2 * E, :]))
        for side, (copy, ok) in enumerate(((to_next, line > 0), (to_prev, line < total - 1))):
            copy.wait_recv()
            hi, lo = split(pad_rows(jnp.where(ok, halo[it, side], F32(0.0))))
            at = 2 * side * E
            wl[0:MP, at : at + E] = hi
            wl[MP:, at : at + E] = lo
            nsum = nsum + fold(dot(wl[:, at : at + E], fsel[1, at : at + E, :]))
        hi, lo = split(nsum)
        kh[0:MP] = hi
        kl[0:MP] = lo
        faces = fold(dot(cl[...], kh[...])) + dot(cl[0:MP], kl[...])
        v[it + 1] = keep * (base - faces)[:MT]

    def gram(pairs):
        used = sorted({i for pair in pairs for i in pair})
        acc = {}
        for t in range(MT // 8):
            rows = {i: v[i, 8 * t : 8 * t + 8, :] for i in used}
            cut = {i: halves(rows[i]) for i in used}
            for a, b in pairs:
                prod, err = two_prod(rows[a], rows[b], cut[a], cut[b])
                if t == 0:
                    acc[a, b] = prod, err
                else:
                    s, e = two_sum(acc[a, b][0], prod)
                    acc[a, b] = s, acc[a, b][1] + (e + err)
        sums = []
        for pair in pairs:
            hi, lo = acc[pair]
            s, e = two_sum(hi[:, :128], hi[:, 128:])
            hi, lo = s, lo[:, :128] + lo[:, 128:] + e
            sums.append(roll_sum(hi, lo, 0, (4, 2, 1)))
        return sums

    def roll_sum(hi, lo, axis, shifts):
        for shift in shifts:
            s, e = two_sum(hi, pltpu.roll(hi, shift, axis))
            lo = lo + pltpu.roll(lo, shift, axis) + e
            hi = s
        return hi, lo

    reb_copies = [
        start(remote(rebg.at[pl.ds(0, 1)], rebg.at[pl.ds(o, 1)], reb_s.at[o - 1], reb_r.at[o - 1], group_dev(o)))
        for o in near
    ]
    coarse_copies = send_coarse(0)
    inputs[4].wait()
    nb_copies = [
        start(remote(nb, nbg.at[0], nb_s.at[0], nb_r.at[0], group_dev(1))),
        start(remote(nb, nbg.at[1], nb_s.at[1], nb_r.at[1], group_dev(-1))),
    ]
    block = send_block(0)
    tell(0)
    apply_both(0, block, coarse_copies, nb_copies)
    coarse_rows(1)
    coarse_copies = send_coarse(1)
    block = send_block(1)
    early = gram(((0, 0), (0, 1), (1, 1)))
    apply_both(1, block, coarse_copies, [])
    late = gram(((0, 2), (1, 2), (2, 2)))

    row, lane = iota((8, 128), 0), iota((8, 128), 1)

    def tree(x):
        err = None
        while x.shape[0] > 8:
            n = x.shape[0] // 2
            x, e = two_sum(x[:n], x[n:])
            err = e if err is None else err[:n] + err[n:] + e
        for shift in (4, 2, 1):
            x, e = two_sum(x, pltpu.roll(x, shift, 0))
            err = e if err is None else err + pltpu.roll(err, shift, 0) + e
        return x, err

    def carry(x, err):
        at = iota(x.shape, 1)
        return x + pltpu.roll(jnp.where(at < 8, err, F32(0.0)), 8, 1)

    hi = jnp.zeros((8, 128), F32)
    lo = jnp.zeros((8, 128), F32)
    for i, (h, l) in enumerate(early + late):
        hi = jnp.where(row == i, h, hi)
        lo = jnp.where(row == i, l, lo)
    rest = jnp.zeros((112, 128), F32)
    total_row = carry(*tree(jnp.concatenate([hi, lo, rest], axis=0).T))

    hear(2)
    def plane_hops(o):
        return min(o % 8, 8 - o % 8) // 2 + min(o // 8, n_y - o // 8)

    def z_hops(o):
        return min(o, n_z - o)

    base = 0
    for stage, (count, target, hops) in enumerate(((8 * n_y, plane_dev, plane_hops), (n_z, z_dev, z_hops))):
        rsrc[stage, 0:1, :] = total_row[0:1]
        copies = []
        for o in sorted(range(1, count), key=lambda o: -hops(o)):
            copies.append(
                start(
                    remote(
                        rsrc.at[stage, pl.ds(0, 1)],
                        red.at[stage, pl.ds(o, 1)],
                        red_s.at[base + o - 1],
                        red_r.at[base + o - 1],
                        target(o),
                    )
                )
            )
        red[stage, 0:1, :] = total_row[0:1]
        base += count - 1
        for copy in copies:
            copy.wait_recv()
        total_row = carry(*tree(red[stage]))

    def pick(i):
        return two_sum(total_row[:, i : i + 1], total_row[:, i + 8 : i + 9])

    g01, g11, g02, g12, g22 = (pick(i) for i in range(1, 6))
    q = dd_div(g12, g11)
    top = dd_add(g02, dd_neg(dd_mul(q, g01)))
    bottom = dd_add(g22, dd_neg(dd_mul(q, g12)))
    beta = (top[0] + top[1]) / (bottom[0] + bottom[1])
    rest = dd_add(g01, dd_neg(dd_mul((beta, jnp.zeros_like(beta)), g12)))
    alpha = (rest[0] + rest[1]) / (g11[0] + g11[1])
    out[...] = alpha[0:1] * z[0, 0:M, :] + beta[0:1] * z[1, 0:M, :]
    for copy in pending:
        copy.wait_send()


def solution(mesh):
    n_wide = mesh.shape["wide"]
    n_z = 16 if n_wide == 64 else n_wide
    n_y = n_wide // n_z

    def per_device(right_side, orders, elem_scale, neighbours, rebalance, mode_diag, stiffness, coupling, block_inverse):
        hbm = pl.BlockSpec(memory_space=pltpu.HBM)
        dma = pltpu.SemaphoreType.DMA
        n_red = 8 * n_y - 1 + n_z - 1
        return pl.pallas_call(
            functools.partial(kernel, (n_wide, n_y, n_z)),
            out_shape=pltpu.VMEM((M, E), F32),
            in_specs=[hbm] * 9,
            out_specs=pl.BlockSpec(memory_space=pltpu.VMEM),
            scratch_shapes=[
                pltpu.VMEM((M, E), F32),
                pltpu.VMEM((1, E), jnp.int32),
                pltpu.VMEM((1, E), F32),
                pltpu.VMEM((4, E), jnp.int32),
                pltpu.VMEM((1, M), F32),
                pltpu.VMEM((M, M), F32),
                pltpu.VMEM((M, M), F32),
                pltpu.VMEM((ORDERS, M, M), F32),
                pltpu.VMEM((3, MT, E), F32),
                pltpu.VMEM((2, 3, MT, E), F32),
                pltpu.VMEM((2, MT, E), F32),
                pltpu.VMEM((2, 2, MT, E), F32),
                pltpu.VMEM((8, E), jnp.int32),
                pltpu.VMEM((8, E), jnp.int32),
                pltpu.VMEM((2, MT, E), F32),
                pltpu.VMEM((2, MT, E), F32),
                pltpu.VMEM((2, 5, 8, E), F32),
                pltpu.VMEM((2, 4, E), jnp.int32),
                pltpu.VMEM((2, 8, 128), F32),
                pltpu.VMEM((2, 32, 128), F32),
                pltpu.VMEM((9, MP, 128), F32),
                pltpu.VMEM((2, 8, 128), F32),
                pltpu.VMEM((2 * MP, ORDERS * 128), BF16),
                pltpu.VMEM((2 * MP, 128), BF16),
                pltpu.VMEM((2 * MP, 128), BF16),
                pltpu.VMEM((4 * E, 2 * E), BF16),
                pltpu.VMEM((3, 3 * E, E), BF16),
                pltpu.VMEM((2 * MP, 4 * E), BF16),
                pltpu.VMEM((2 * MP, 3 * E), BF16),
                pltpu.VMEM((ORDERS * 128, E), BF16),
                pltpu.VMEM((ORDERS * 128, E), BF16),
                pltpu.VMEM((128, E), BF16),
                pltpu.VMEM((128, E), BF16),
                dma((9,)),
                dma((2, 3)),
                dma((2, 3)),
                dma,
                dma,
                dma((2,)),
                dma((2,)),
                dma((7,)),
                dma((7,)),
                dma((2, 4)),
                dma((2, 4)),
                dma((2,)),
                dma((2,)),
                dma((2, 2)),
                dma((2, 2)),
                dma((n_red,)),
                dma((n_red,)),
                pltpu.SemaphoreType.REGULAR((3,)),
            ],
            compiler_params=pltpu.CompilerParams(
                collective_id=0, has_side_effects=True, vmem_limit_bytes=60 * 1024 * 1024
            ),
        )(
            right_side,
            orders.reshape(1, E),
            elem_scale.reshape(1, E),
            neighbours,
            rebalance.reshape(1, E),
            mode_diag.reshape(1, M),
            stiffness,
            coupling,
            block_inverse,
        )

    line = ("wide", "narrow", "chip")
    return jax.shard_map(
        per_device,
        mesh=mesh,
        in_specs=(P(None, line), P(line), P(line), P(None, line), P(line), P(), P(), P(), P()),
        out_specs=P(None, line),
        check_vma=False,
    )
```

```python
import functools

import jax
import jax.numpy as jnp
from jax import lax
from jax.experimental import pallas as pl
from jax.experimental.pallas import tpu as pltpu
from jax.sharding import PartitionSpec as P

M = 100
MT = 104
MP = 112
E = 256
ORDERS = 6
MIN_ORDER = 4
SHIFT = 0.5
COARSE = (0, 1, 10, 11)
MESH = pl.DeviceIdType.MESH
F32 = jnp.float32
BF16 = jnp.bfloat16


def two_sum(a, b):
    s = a + b
    t = s - a
    return s, (a - (s - t)) + (b - t)


def halves(a):
    t = a * F32(4097.0)
    hi = t - (t - a)
    return hi, a - hi


def two_prod(a, b, a_parts=None, b_parts=None):
    ah, al = halves(a) if a_parts is None else a_parts
    bh, bl = halves(b) if b_parts is None else b_parts
    p = a * b
    return p, ((ah * bh - p) + ah * bl + al * bh) + al * bl


def split(x):
    hi = x.astype(BF16)
    return hi, (x - hi.astype(F32)).astype(BF16)


def dot(a, b):
    return jnp.dot(a, b, preferred_element_type=F32)


def iota(shape, axis):
    return lax.broadcasted_iota(jnp.int32, shape, axis)


def pad_rows(x):
    return jnp.concatenate([x, jnp.zeros((MP - MT, x.shape[1]), F32)], axis=0)


def fold(d):
    return d[:MP] + d[MP:]


def kernel(
    sizes,
    rs_h, ords_h, scale_h, nb_h, reb_h, diag_h, st_h, cp_h, bi_h, out,
    rs, ords, scale, nb, diag, st, cp, bi,
    v, ag, z, halo, rebg, prow, give, take, cw, nbg, rsrc, red, pad, cpad,
    bl, sl, cl, tsel, fsel, gl, wl, mh, ml, kh, kl, chosen,
    in_s, ag_s, ag_r, pr_s, pr_r, give_s, give_r, reb_s, reb_r, cw_s, cw_r, nb_s, nb_r,
    halo_s, halo_r, red_s, red_r, known,
):
    n_wide, n_y, n_z = sizes
    w, x, c = lax.axis_index("wide"), lax.axis_index("narrow"), lax.axis_index("chip")
    p = 2 * x + c
    line = w * 8 + p
    total = n_wide * 8
    wy, wz = lax.div(w, n_z), lax.rem(w, n_z)

    def group_dev(off):
        q = lax.rem(p + (off + 8), 8)
        return (w, lax.div(q, 2), lax.rem(q, 2))

    def line_dev(off):
        q = lax.rem(line + (off + total), total)
        return (lax.div(q, 8), lax.div(lax.rem(q, 8), 2), lax.rem(q, 2))

    def plane_dev(off):
        q = lax.rem(p + off % 8, 8)
        return (lax.rem(wy + off // 8, n_y) * n_z + wz, lax.div(q, 2), lax.rem(q, 2))

    def z_dev(off):
        return (wy * n_z + lax.rem(wz + (off + n_z), n_z), x, c)

    def both_ways(off):
        return [z_dev(off)] if 2 * off == n_z else [z_dev(off), z_dev(-off)]

    right, left = (w, lax.rem(x + 1, 4), c), (w, lax.rem(x + 3, 4), c)
    across, sib = (w, lax.rem(x + 2, 4), c), (w, x, 1 - c)

    inputs = [
        pltpu.make_async_copy(src, dst, in_s.at[i])
        for i, (src, dst) in enumerate(
            (
                (rs_h, rs), (ords_h, ords), (scale_h, scale), (reb_h, rebg.at[pl.ds(0, 1)]),
                (nb_h, nb), (diag_h, diag), (st_h, st), (cp_h, cp), (bi_h, bi),
            )
        )
    ]
    for copy in inputs[:4]:
        copy.start()

    barrier = pltpu.get_barrier_semaphore()
    near = (4, 3, 5, 2, 6, 1, 7)
    columns = [plane_dev(8 * o) for o in sorted(range(1, n_y), key=lambda o: -min(o, n_y - o))]
    greeted = columns + [line_dev(1), line_dev(-1)] + [group_dev(o) for o in near] + both_ways(1)
    for d in greeted:
        pl.semaphore_signal(barrier, inc=1, device_id=d, device_id_type=MESH)
    for copy in inputs[4:]:
        copy.start()

    rounds = [columns + both_ways(1)] + [both_ways(o) for o in (2, 4) if 2 * o < n_z]

    def tell(i):
        if i < len(rounds):
            for d in rounds[i]:
                pl.semaphore_signal(known.at[i], inc=1, device_id=d, device_id_type=MESH)

    def hear(i):
        if i < len(rounds):
            pl.semaphore_wait(known.at[i], len(rounds[i]))

    mode = iota((MT, E), 0)
    row_degree = (mode * 103) >> 10
    degree = jnp.maximum(row_degree, mode - 10 * row_degree)
    v[0, 96:MT, :] = jnp.zeros((8, E), F32)
    for copy in inputs[:4]:
        copy.wait()
    kept = jnp.where(degree <= ords[...], F32(1.0), F32(0.0))
    v[0, 0:M, :] = kept[0:M] * rs[...]
    for it in range(2):
        cw[it, 2] = jnp.zeros((8, E), F32)
        cw[it, 2, 4:5, :] = scale[...]

    def coarse_rows(it):
        cw[it, 2, 0:2, :] = v[it, 0:2, :]
        cw[it, 2, 2:4, :] = v[it, 10:12, :]

    coarse_rows(0)
    for stage, count in enumerate((8 * n_y, n_z)):
        if count < 32:
            red[stage, count:32, :] = jnp.zeros((32 - count, 128), F32)
    pl.semaphore_wait(barrier, len(greeted))

    def remote(src, dst, ssem, rsem, d):
        return pltpu.make_async_remote_copy(
            src_ref=src, dst_ref=dst, send_sem=ssem, recv_sem=rsem, device_id=d, device_id_type=MESH
        )

    pending = []

    def start(copy):
        copy.start()
        pending.append(copy)
        return copy

    def send_coarse(it):
        copies = []
        for i, o in enumerate((1, -1, 2, -2)):
            copies.append(
                start(remote(cw.at[it, 2], cw.at[it, 2 - o], cw_s.at[it, i], cw_r.at[it, i], group_dev(o)))
            )
        return copies

    def send_block(it):
        copies = [
            start(remote(v.at[it], ag.at[it, i], ag_s.at[it, i], ag_r.at[it, i], d))
            for i, d in ((0, right), (1, left), (2, across))
        ]
        return copies

    offsets = (0, 3, 1, 2)

    def put_block(it, b):
        hi, lo = split(pad_rows(v[it] if b == 0 else ag[it, b - 1]))
        gl[0:MP, b * E : (b + 1) * E] = hi
        gl[MP:, b * E : (b + 1) * E] = lo

    def gather(b0, b1, half):
        return fold(dot(gl[:, b0 * E : b1 * E], tsel[b0 * E : b1 * E, half * E : (half + 1) * E]))

    def prepare_matrices():
        for copy in inputs[5:]:
            copy.wait()
        pad[...] = jnp.zeros(pad.shape, F32)
        for o in range(ORDERS):
            pad[o, 0:M, 0:M] = bi[o]
        pad[6, 0:M, 0:M] = st[...]
        pad[7, 0:M, 0:M] = F32(0.25) * cp[...]
        pad[8, 0:1, 0:M] = diag[...]
        for o in range(ORDERS):
            hi, lo = split(pad[o])
            bl[0:MP, o * 128 : (o + 1) * 128] = hi
            bl[MP:, o * 128 : (o + 1) * 128] = lo
        s = pad[6]
        s = s + jnp.where(iota((MP, 128), 0) == iota((MP, 128), 1), pad[8, 0:1, :], F32(0.0))
        hi, lo = split(s)
        sl[0:MP] = hi
        sl[MP:] = lo
        pad[6] = s
        hi, lo = split(pad[7])
        cl[0:MP] = hi
        cl[MP:] = lo
        cpad[...] = jnp.zeros(cpad.shape, F32)
        for i in range(2):
            cpad[i, 0:2, :] = pad[6 + i, 0:2, :]
            cpad[i, 2:4, :] = pad[6 + i, 10:12, :]
        for ref in (kh, kl):
            ref[MP:128] = jnp.zeros((16, E), BF16)
        for o in range(ORDERS):
            chosen[o] = jnp.where(
                jnp.broadcast_to(ords[...], (MP, E)) == o + MIN_ORDER, F32(1.0), F32(0.0)
            ).astype(BF16)
            for ref in (mh, ml):
                ref[o * 128 + MP : (o + 1) * 128] = jnp.zeros((16, E), BF16)

    def partner_table():
        rows = rebg[...]
        even = iota((8, E), 1) % 2 == 0
        swapped = jnp.where(even, pltpu.roll(rows, E - 1, 1), pltpu.roll(rows, 1, 1)).astype(F32)
        me = iota((E, 128), 0) + p * E
        acc = jnp.zeros((E, 128), F32)
        for s in range(8):
            for h in range(2):
                lanes = slice(h * 128, (h + 1) * 128)
                acc = acc + jnp.where(rows[s : s + 1, lanes] == me, swapped[s : s + 1, lanes], F32(0.0))
        column = jnp.sum(acc, axis=1, keepdims=True)
        partner = jnp.sum(
            jnp.where(iota((E, E), 0) == iota((E, E), 1), column, F32(0.0)), axis=0, keepdims=True
        ).astype(jnp.int32)
        prow[0:1, :] = partner
        swap = start(remote(prow.at[pl.ds(0, 1)], prow.at[pl.ds(1, 1)], pr_s, pr_r, sib))
        for half in range(2):
            if half == 1:
                swap.wait_recv()
            for b, r in enumerate(offsets):
                local = prow[half : half + 1, :] - (2 * lax.rem(x + r, 4) + c) * E

                @pl.loop(0, E // 64)
                def _(i):
                    hit = iota((64, E), 0) + i * 64 == local
                    tsel[pl.ds(b * E + i * 64, 64), half * E : (half + 1) * E] = jnp.where(
                        hit, F32(1.0), F32(0.0)
                    ).astype(BF16)

    def face_table(slot, index):
        @pl.loop(0, 3 * E // 64)
        def _(i):
            here = iota((64, E), 0) + i * 64
            count = jnp.zeros((64, E), F32)
            for f in range(4):
                count = count + jnp.where(here == index[f], F32(1.0), F32(0.0))
            fsel[slot, pl.ds(i * 64, 64), :] = count.astype(BF16)

    def coarse_solve(it):
        row = iota((8, E), 0)
        stiff = cpad[0]
        gain = cpad[1]
        s_col = [stiff[:, m : m + 1] for m in COARSE]
        g_col = [gain[:, m : m + 1] for m in COARSE]
        row1 = iota((8, 1), 0)
        dsum = jnp.zeros((8, 1), F32)
        for j in range(4):
            dsum = dsum + jnp.where(row1 == j, s_col[j], F32(0.0))
        rhs, scales, inverse, valid, y = [], [], [], [], []
        for o in range(-2, 3):
            ok = jnp.logical_and(p + o >= 0, p + o < 8)
            block = jnp.where(ok, cw[it, o + 2], F32(0.0))
            rhs.append(jnp.where(row < 4, block, F32(0.0)))
            scales.append(block[4:5])
            inverse.append(F32(1.0) / (block[4:5] * dsum - F32(SHIFT)))
            valid.append(ok)
            y.append(inverse[-1] * rhs[-1])

        def update(i, slot, y):
            window = jnp.concatenate([y[i - 1], y[i], y[i + 1]], axis=1)
            hi = window.astype(BF16).astype(F32)
            both = jnp.concatenate([hi, window - hi], axis=0).astype(BF16)
            d = dot(both, fsel[slot])
            nsum = d[0:8] + d[8:16]
            own = jnp.zeros((8, E), F32)
            faces = jnp.zeros((8, E), F32)
            for j in range(4):
                own = own + s_col[j] * y[i][j : j + 1]
                faces = faces + g_col[j] * nsum[j : j + 1]
            image = scales[i] * own - F32(SHIFT) * y[i] - faces
            new = y[i] + inverse[i] * (rhs[i] - image)
            return jnp.where(valid[i], new, F32(0.0))

        first = [None] + [update(i, i - 1, y) for i in (1, 2, 3)]
        return update(2, 1, first)

    def smooth(mixed):
        hi, lo = split(mixed)
        for o in range(ORDERS):
            mh[o * 128 : o * 128 + MP] = hi * chosen[o]
            ml[o * 128 : o * 128 + MP] = lo * chosen[o]
        return fold(dot(bl[...], mh[...])) + dot(bl[0:MP], ml[...])

    def apply_both(it, block, coarse_copies, nb_copies):
        if it == 0:
            for copy in reb_copies:
                copy.wait_recv()
            partner_table()
            prepare_matrices()
            face_table(1, [nb[f : f + 1, :] for f in range(4)])
            for copy in nb_copies:
                copy.wait_recv()
            face_table(0, [nbg[0, f : f + 1, :] for f in range(4)])
            face_table(2, [nbg[1, f : f + 1, :] for f in range(4)])
        put_block(it, 0)
        for copy in coarse_copies:
            copy.wait_recv()
        coarse = coarse_solve(it)
        block[0].wait_recv()
        put_block(it, 1)
        block[1].wait_recv()
        put_block(it, 2)
        theirs = gather(0, 3, 1)
        block[2].wait_recv()
        put_block(it, 3)
        theirs = theirs + gather(3, 4, 1)
        give[it] = theirs[:MT]
        handed = start(remote(give.at[it], take.at[it], give_s.at[it], give_r.at[it], sib))
        mine = gather(0, 4, 0)
        handed.wait_recv()
        mixed = pad_rows(v[it] + F32(0.5) * (mine[:MT] + take[it]))
        keep = jnp.where(degree <= ords[...], F32(1.0), F32(0.0))
        z[it] = keep * smooth(mixed)[:MT]
        z[it, 0:2, :] = z[it, 0:2, :] + coarse[0:2]
        z[it, 10:12, :] = z[it, 10:12, :] + coarse[2:4]

        to_next = start(remote(z.at[it], halo.at[it, 0], halo_s.at[it, 0], halo_r.at[it, 0], line_dev(1)))
        to_prev = start(remote(z.at[it], halo.at[it, 1], halo_s.at[it, 1], halo_r.at[it, 1], line_dev(-1)))

        hear(it)
        tell(it + 1)
        zv = pad_rows(z[it])
        hi, lo = split(zv)
        wl[0:MP, E : 2 * E] = hi
        wl[MP:, E : 2 * E] = lo
        kh[0:MP] = hi
        kl[0:MP] = lo
        own = fold(dot(sl[...], kh[...])) + dot(sl[0:MP], kl[...])
        base = scale[...] * own - F32(SHIFT) * zv
        nsum = fold(dot(wl[:, E : 2 * E], fsel[1, E : 2 * E, :]))
        for side, (copy, ok) in enumerate(((to_next, line > 0), (to_prev, line < total - 1))):
            copy.wait_recv()
            hi, lo = split(pad_rows(jnp.where(ok, halo[it, side], F32(0.0))))
            at = 2 * side * E
            wl[0:MP, at : at + E] = hi
            wl[MP:, at : at + E] = lo
            nsum = nsum + fold(dot(wl[:, at : at + E], fsel[1, at : at + E, :]))
        hi, lo = split(nsum)
        kh[0:MP] = hi
        kl[0:MP] = lo
        faces = fold(dot(cl[...], kh[...])) + dot(cl[0:MP], kl[...])
        v[it + 1] = keep * (base - faces)[:MT]

    def gram(pairs):
        used = sorted({i for pair in pairs for i in pair})
        acc = {}
        for t in range(MT // 8):
            rows = {i: v[i, 8 * t : 8 * t + 8, :] for i in used}
            cut = {i: halves(rows[i]) for i in used}
            for a, b in pairs:
                prod, err = two_prod(rows[a], rows[b], cut[a], cut[b])
                if t == 0:
                    acc[a, b] = prod, err
                else:
                    s, e = two_sum(acc[a, b][0], prod)
                    acc[a, b] = s, acc[a, b][1] + (e + err)
        sums = []
        for pair in pairs:
            hi, lo = acc[pair]
            s, e = two_sum(hi[:, :128], hi[:, 128:])
            hi, lo = s, lo[:, :128] + lo[:, 128:] + e
            sums.append(roll_sum(hi, lo, 0, (4, 2, 1)))
        return sums

    def roll_sum(hi, lo, axis, shifts):
        for shift in shifts:
            s, e = two_sum(hi, pltpu.roll(hi, shift, axis))
            lo = lo + pltpu.roll(lo, shift, axis) + e
            hi = s
        return hi, lo

    reb_copies = [
        start(remote(rebg.at[pl.ds(0, 1)], rebg.at[pl.ds(o, 1)], reb_s.at[o - 1], reb_r.at[o - 1], group_dev(o)))
        for o in near
    ]
    coarse_copies = send_coarse(0)
    inputs[4].wait()
    nb_copies = [
        start(remote(nb, nbg.at[0], nb_s.at[0], nb_r.at[0], group_dev(1))),
        start(remote(nb, nbg.at[1], nb_s.at[1], nb_r.at[1], group_dev(-1))),
    ]
    block = send_block(0)
    tell(0)
    apply_both(0, block, coarse_copies, nb_copies)
    coarse_rows(1)
    coarse_copies = send_coarse(1)
    block = send_block(1)
    early = gram(((0, 0), (0, 1), (1, 1)))
    apply_both(1, block, coarse_copies, [])
    late = gram(((0, 2), (1, 2), (2, 2)))

    row, lane = iota((8, 128), 0), iota((8, 128), 1)

    def tree(x):
        err = None
        while x.shape[0] > 8:
            n = x.shape[0] // 2
            x, e = two_sum(x[:n], x[n:])
            err = e if err is None else err[:n] + err[n:] + e
        for shift in (4, 2, 1):
            x, e = two_sum(x, pltpu.roll(x, shift, 0))
            err = e if err is None else err + pltpu.roll(err, shift, 0) + e
        return x, err

    def carry(x, err):
        at = iota(x.shape, 1)
        return x + pltpu.roll(jnp.where(at < 8, err, F32(0.0)), 8, 1)

    hi = jnp.zeros((8, 128), F32)
    lo = jnp.zeros((8, 128), F32)
    for i, (h, l) in enumerate(early + late):
        hi = jnp.where(row == i, h, hi)
        lo = jnp.where(row == i, l, lo)
    rest = jnp.zeros((112, 128), F32)
    total_row = carry(*tree(jnp.concatenate([hi, lo, rest], axis=0).T))

    hear(2)
    def plane_hops(o):
        return min(o % 8, 8 - o % 8) // 2 + min(o // 8, n_y - o // 8)

    def z_hops(o):
        return min(o, n_z - o)

    base = 0
    for stage, (count, target, hops) in enumerate(((8 * n_y, plane_dev, plane_hops), (n_z, z_dev, z_hops))):
        rsrc[stage, 0:1, :] = total_row[0:1]
        copies = []
        for o in sorted(range(1, count), key=lambda o: -hops(o)):
            copies.append(
                start(
                    remote(
                        rsrc.at[stage, pl.ds(0, 1)],
                        red.at[stage, pl.ds(o, 1)],
                        red_s.at[base + o - 1],
                        red_r.at[base + o - 1],
                        target(o),
                    )
                )
            )
        red[stage, 0:1, :] = total_row[0:1]
        base += count - 1
        for copy in copies:
            copy.wait_recv()
        total_row = carry(*tree(red[stage]))

    def pick(i):
        return (pltpu.roll(total_row, 128 - i, 1) if i else total_row), pltpu.roll(total_row, 120 - i, 1)

    def less(a, factor, b):
        p, e = two_prod(factor, b[0])
        s, t = two_sum(a[0], -p)
        return s, (t - e) + (a[1] - factor * b[1])

    g01, g11, g02, g12, g22 = (pick(i) for i in range(1, 6))
    inverse = F32(1.0) / g11[0]
    q = g12[0] * inverse
    left_over = less(g12, q, g11)
    q_low = (left_over[0] + left_over[1]) * inverse
    top = less(g02, q, g01)
    bottom = less(g22, q, g12)
    beta = (top[0] + (top[1] - q_low * g01[0])) / (bottom[0] + (bottom[1] - q_low * g12[0]))
    rest = less(g01, beta, g12)
    alpha = (rest[0] + rest[1]) * inverse
    alpha, beta = alpha[0:1, 0:1], beta[0:1, 0:1]
    out[...] = alpha * z[0, 0:M, :] + beta * z[1, 0:M, :]
    for copy in pending:
        copy.wait_send()


def solution(mesh):
    n_wide = mesh.shape["wide"]
    n_z = 16 if n_wide == 64 else n_wide
    n_y = n_wide // n_z

    def per_device(right_side, orders, elem_scale, neighbours, rebalance, mode_diag, stiffness, coupling, block_inverse):
        hbm = pl.BlockSpec(memory_space=pltpu.HBM)
        dma = pltpu.SemaphoreType.DMA
        n_red = 8 * n_y - 1 + n_z - 1
        return pl.pallas_call(
            functools.partial(kernel, (n_wide, n_y, n_z)),
            out_shape=pltpu.VMEM((M, E), F32),
            in_specs=[hbm] * 9,
            out_specs=pl.BlockSpec(memory_space=pltpu.VMEM),
            scratch_shapes=[
                pltpu.VMEM((M, E), F32),
                pltpu.VMEM((1, E), jnp.int32),
                pltpu.VMEM((1, E), F32),
                pltpu.VMEM((4, E), jnp.int32),
                pltpu.VMEM((1, M), F32),
                pltpu.VMEM((M, M), F32),
                pltpu.VMEM((M, M), F32),
                pltpu.VMEM((ORDERS, M, M), F32),
                pltpu.VMEM((3, MT, E), F32),
                pltpu.VMEM((2, 3, MT, E), F32),
                pltpu.VMEM((2, MT, E), F32),
                pltpu.VMEM((2, 2, MT, E), F32),
                pltpu.VMEM((8, E), jnp.int32),
                pltpu.VMEM((8, E), jnp.int32),
                pltpu.VMEM((2, MT, E), F32),
                pltpu.VMEM((2, MT, E), F32),
                pltpu.VMEM((2, 5, 8, E), F32),
                pltpu.VMEM((2, 4, E), jnp.int32),
                pltpu.VMEM((2, 8, 128), F32),
                pltpu.VMEM((2, 32, 128), F32),
                pltpu.VMEM((9, MP, 128), F32),
                pltpu.VMEM((2, 8, 128), F32),
                pltpu.VMEM((2 * MP, ORDERS * 128), BF16),
                pltpu.VMEM((2 * MP, 128), BF16),
                pltpu.VMEM((2 * MP, 128), BF16),
                pltpu.VMEM((4 * E, 2 * E), BF16),
                pltpu.VMEM((3, 3 * E, E), BF16),
                pltpu.VMEM((2 * MP, 4 * E), BF16),
                pltpu.VMEM((2 * MP, 3 * E), BF16),
                pltpu.VMEM((ORDERS * 128, E), BF16),
                pltpu.VMEM((ORDERS * 128, E), BF16),
                pltpu.VMEM((128, E), BF16),
                pltpu.VMEM((128, E), BF16),
                pltpu.VMEM((ORDERS, MP, E), BF16),
                dma((9,)),
                dma((2, 3)),
                dma((2, 3)),
                dma,
                dma,
                dma((2,)),
                dma((2,)),
                dma((7,)),
                dma((7,)),
                dma((2, 4)),
                dma((2, 4)),
                dma((2,)),
                dma((2,)),
                dma((2, 2)),
                dma((2, 2)),
                dma((n_red,)),
                dma((n_red,)),
                pltpu.SemaphoreType.REGULAR((3,)),
            ],
            compiler_params=pltpu.CompilerParams(
                collective_id=0, has_side_effects=True, vmem_limit_bytes=60 * 1024 * 1024
            ),
        )(
            right_side,
            orders.reshape(1, E),
            elem_scale.reshape(1, E),
            neighbours,
            rebalance.reshape(1, E),
            mode_diag.reshape(1, M),
            stiffness,
            coupling,
            block_inverse,
        )

    line = ("wide", "narrow", "chip")
    return jax.shard_map(
        per_device,
        mesh=mesh,
        in_specs=(P(None, line), P(line), P(line), P(None, line), P(line), P(), P(), P(), P()),
        out_specs=P(None, line),
        check_vma=False,
    )
```

```python
import functools

import jax
import jax.numpy as jnp
from jax import lax
from jax.experimental import pallas as pl
from jax.experimental.pallas import tpu as pltpu
from jax.sharding import PartitionSpec as P

M = 100
MT = 104
MP = 112
E = 256
ORDERS = 6
MIN_ORDER = 4
SHIFT = 0.5
COARSE = (0, 1, 10, 11)
MESH = pl.DeviceIdType.MESH
F32 = jnp.float32
BF16 = jnp.bfloat16


def two_sum(a, b):
    s = a + b
    t = s - a
    return s, (a - (s - t)) + (b - t)


def halves(a):
    t = a * F32(4097.0)
    hi = t - (t - a)
    return hi, a - hi


def two_prod(a, b, a_parts=None, b_parts=None):
    ah, al = halves(a) if a_parts is None else a_parts
    bh, bl = halves(b) if b_parts is None else b_parts
    p = a * b
    return p, ((ah * bh - p) + ah * bl + al * bh) + al * bl


def split(x):
    hi = x.astype(BF16)
    return hi, (x - hi.astype(F32)).astype(BF16)


def dot(a, b):
    return jnp.dot(a, b, preferred_element_type=F32)


def iota(shape, axis):
    return lax.broadcasted_iota(jnp.int32, shape, axis)


def pad_rows(x):
    return jnp.concatenate([x, jnp.zeros((MP - MT, x.shape[1]), F32)], axis=0)


def fold(d):
    return d[:MP] + d[MP:]


def kernel(
    sizes,
    rs_h, ords_h, scale_h, nb_h, reb_h, diag_h, st_h, cp_h, bi_h, out,
    rs, ords, scale, nb, diag, st, cp, bi,
    v, ag, z, halo, rebg, prow, give, take, cw, nbg, rsrc, red, pad, cpad,
    bl, sl, cl, tsel, fsel, gl, wl, mh, ml, kh, kl, chosen,
    in_s, ag_s, ag_r, pr_s, pr_r, give_s, give_r, reb_s, reb_r, cw_s, cw_r, nb_s, nb_r,
    halo_s, halo_r, red_s, red_r, known,
):
    n_wide, n_y, n_z = sizes
    w, x, c = lax.axis_index("wide"), lax.axis_index("narrow"), lax.axis_index("chip")
    p = 2 * x + c
    line = w * 8 + p
    total = n_wide * 8
    wy, wz = lax.div(w, n_z), lax.rem(w, n_z)

    def group_dev(off):
        q = lax.rem(p + (off + 8), 8)
        return (w, lax.div(q, 2), lax.rem(q, 2))

    def line_dev(off):
        q = lax.rem(line + (off + total), total)
        return (lax.div(q, 8), lax.div(lax.rem(q, 8), 2), lax.rem(q, 2))

    def plane_dev(off):
        q = lax.rem(p + off % 8, 8)
        return (lax.rem(wy + off // 8, n_y) * n_z + wz, lax.div(q, 2), lax.rem(q, 2))

    def z_dev(off):
        return (wy * n_z + lax.rem(wz + (off + n_z), n_z), x, c)

    def both_ways(off):
        return [z_dev(off)] if 2 * off == n_z else [z_dev(off), z_dev(-off)]

    right, left = (w, lax.rem(x + 1, 4), c), (w, lax.rem(x + 3, 4), c)
    across, sib = (w, lax.rem(x + 2, 4), c), (w, x, 1 - c)

    inputs = [
        pltpu.make_async_copy(src, dst, in_s.at[i])
        for i, (src, dst) in enumerate(
            (
                (rs_h, rs), (ords_h, ords), (scale_h, scale), (reb_h, rebg.at[pl.ds(0, 1)]),
                (nb_h, nb), (diag_h, diag), (st_h, st), (cp_h, cp), (bi_h, bi),
            )
        )
    ]
    for copy in inputs[:4]:
        copy.start()

    barrier = pltpu.get_barrier_semaphore()
    near = (4, 3, 5, 2, 6, 1, 7)
    columns = [plane_dev(8 * o) for o in sorted(range(1, n_y), key=lambda o: -min(o, n_y - o))]
    greeted = columns + [line_dev(1), line_dev(-1)] + [group_dev(o) for o in near] + both_ways(1)
    for d in greeted:
        pl.semaphore_signal(barrier, inc=1, device_id=d, device_id_type=MESH)
    for copy in inputs[4:]:
        copy.start()

    rounds = [columns + both_ways(1)] + [both_ways(o) for o in (2, 4) if 2 * o < n_z]

    def tell(i):
        if i < len(rounds):
            for d in rounds[i]:
                pl.semaphore_signal(known.at[i], inc=1, device_id=d, device_id_type=MESH)

    def hear(i):
        if i < len(rounds):
            pl.semaphore_wait(known.at[i], len(rounds[i]))

    mode = iota((MT, E), 0)
    row_degree = (mode * 103) >> 10
    degree = jnp.maximum(row_degree, mode - 10 * row_degree)
    v[0, 96:MT, :] = jnp.zeros((8, E), F32)
    for copy in inputs[:4]:
        copy.wait()
    kept = jnp.where(degree <= ords[...], F32(1.0), F32(0.0))
    v[0, 0:M, :] = kept[0:M] * rs[...]
    for it in range(2):
        cw[it, 2] = jnp.zeros((8, E), F32)
        cw[it, 2, 4:5, :] = scale[...]

    def coarse_rows(it):
        cw[it, 2, 0:2, :] = v[it, 0:2, :]
        cw[it, 2, 2:4, :] = v[it, 10:12, :]

    coarse_rows(0)
    for stage, count in enumerate((8 * n_y, n_z)):
        if count < 32:
            red[stage, count:32, :] = jnp.zeros((32 - count, 128), F32)
    pl.semaphore_wait(barrier, len(greeted))

    def remote(src, dst, ssem, rsem, d):
        return pltpu.make_async_remote_copy(
            src_ref=src, dst_ref=dst, send_sem=ssem, recv_sem=rsem, device_id=d, device_id_type=MESH
        )

    pending = []

    def start(copy):
        copy.start()
        pending.append(copy)
        return copy

    def settle(count):
        for copy in pending[:count]:
            copy.wait_send()
        del pending[:count]

    def send_coarse(it):
        copies = []
        for i, o in enumerate((1, -1, 2, -2)):
            copies.append(
                start(remote(cw.at[it, 2], cw.at[it, 2 - o], cw_s.at[it, i], cw_r.at[it, i], group_dev(o)))
            )
        return copies

    def send_block(it):
        copies = [
            start(remote(v.at[it], ag.at[it, i], ag_s.at[it, i], ag_r.at[it, i], d))
            for i, d in enumerate((across, right, left))
        ]
        return copies

    offsets = (0, 2, 3, 1)

    def put_block(it, b):
        hi, lo = split(pad_rows(v[it] if b == 0 else ag[it, b - 1]))
        gl[0:MP, b * E : (b + 1) * E] = hi
        gl[MP:, b * E : (b + 1) * E] = lo

    def gather(b0, b1, half):
        return fold(dot(gl[:, b0 * E : b1 * E], tsel[b0 * E : b1 * E, half * E : (half + 1) * E]))

    def prepare_matrices():
        for copy in inputs[5:]:
            copy.wait()
        pad[...] = jnp.zeros(pad.shape, F32)
        for o in range(ORDERS):
            pad[o, 0:M, 0:M] = bi[o]
        pad[6, 0:M, 0:M] = st[...]
        pad[7, 0:M, 0:M] = F32(0.25) * cp[...]
        pad[8, 0:1, 0:M] = diag[...]
        for o in range(ORDERS):
            hi, lo = split(pad[o])
            bl[0:MP, o * 128 : (o + 1) * 128] = hi
            bl[MP:, o * 128 : (o + 1) * 128] = lo
        s = pad[6]
        s = s + jnp.where(iota((MP, 128), 0) == iota((MP, 128), 1), pad[8, 0:1, :], F32(0.0))
        hi, lo = split(s)
        sl[0:MP] = hi
        sl[MP:] = lo
        pad[6] = s
        hi, lo = split(pad[7])
        cl[0:MP] = hi
        cl[MP:] = lo
        cpad[...] = jnp.zeros(cpad.shape, F32)
        for i in range(2):
            cpad[i, 0:2, :] = pad[6 + i, 0:2, :]
            cpad[i, 2:4, :] = pad[6 + i, 10:12, :]
        for ref in (kh, kl):
            ref[MP:128] = jnp.zeros((16, E), BF16)
        for o in range(ORDERS):
            chosen[o] = jnp.where(
                jnp.broadcast_to(ords[...], (MP, E)) == o + MIN_ORDER, F32(1.0), F32(0.0)
            ).astype(BF16)
            for ref in (mh, ml):
                ref[o * 128 + MP : (o + 1) * 128] = jnp.zeros((16, E), BF16)

    def partner_table():
        rows = rebg[...]
        even = iota((8, E), 1) % 2 == 0
        swapped = jnp.where(even, pltpu.roll(rows, E - 1, 1), pltpu.roll(rows, 1, 1)).astype(F32)
        me = iota((E, 128), 0) + p * E
        acc = jnp.zeros((E, 128), F32)
        for s in range(8):
            for h in range(2):
                lanes = slice(h * 128, (h + 1) * 128)
                acc = acc + jnp.where(rows[s : s + 1, lanes] == me, swapped[s : s + 1, lanes], F32(0.0))
        column = jnp.sum(acc, axis=1, keepdims=True)
        partner = jnp.sum(
            jnp.where(iota((E, E), 0) == iota((E, E), 1), column, F32(0.0)), axis=0, keepdims=True
        ).astype(jnp.int32)
        prow[0:1, :] = partner
        swap = start(remote(prow.at[pl.ds(0, 1)], prow.at[pl.ds(1, 1)], pr_s, pr_r, sib))
        for half in range(2):
            if half == 1:
                swap.wait_recv()
            for b, r in enumerate(offsets):
                local = prow[half : half + 1, :] - (2 * lax.rem(x + r, 4) + c) * E

                @pl.loop(0, E // 64)
                def _(i):
                    hit = iota((64, E), 0) + i * 64 == local
                    tsel[pl.ds(b * E + i * 64, 64), half * E : (half + 1) * E] = jnp.where(
                        hit, F32(1.0), F32(0.0)
                    ).astype(BF16)

    def face_table(slot, index):
        @pl.loop(0, 3 * E // 64)
        def _(i):
            here = iota((64, E), 0) + i * 64
            count = jnp.zeros((64, E), F32)
            for f in range(4):
                count = count + jnp.where(here == index[f], F32(1.0), F32(0.0))
            fsel[slot, pl.ds(i * 64, 64), :] = count.astype(BF16)

    def coarse_solve(it):
        row = iota((8, E), 0)
        stiff = cpad[0]
        gain = cpad[1]
        s_col = [stiff[:, m : m + 1] for m in COARSE]
        g_col = [gain[:, m : m + 1] for m in COARSE]
        row1 = iota((8, 1), 0)
        dsum = jnp.zeros((8, 1), F32)
        for j in range(4):
            dsum = dsum + jnp.where(row1 == j, s_col[j], F32(0.0))
        rhs, scales, inverse, valid, y = [], [], [], [], []
        for o in range(-2, 3):
            ok = jnp.logical_and(p + o >= 0, p + o < 8)
            block = jnp.where(ok, cw[it, o + 2], F32(0.0))
            rhs.append(jnp.where(row < 4, block, F32(0.0)))
            scales.append(block[4:5])
            inverse.append(F32(1.0) / (block[4:5] * dsum - F32(SHIFT)))
            valid.append(ok)
            y.append(inverse[-1] * rhs[-1])

        def update(i, slot, y):
            window = jnp.concatenate([y[i - 1], y[i], y[i + 1]], axis=1)
            hi = window.astype(BF16).astype(F32)
            both = jnp.concatenate([hi, window - hi], axis=0).astype(BF16)
            d = dot(both, fsel[slot])
            nsum = d[0:8] + d[8:16]
            own = jnp.zeros((8, E), F32)
            faces = jnp.zeros((8, E), F32)
            for j in range(4):
                own = own + s_col[j] * y[i][j : j + 1]
                faces = faces + g_col[j] * nsum[j : j + 1]
            image = scales[i] * own - F32(SHIFT) * y[i] - faces
            new = y[i] + inverse[i] * (rhs[i] - image)
            return jnp.where(valid[i], new, F32(0.0))

        first = [None] + [update(i, i - 1, y) for i in (1, 2, 3)]
        return update(2, 1, first)

    def smooth(mixed):
        hi, lo = split(mixed)
        for o in range(ORDERS):
            mh[o * 128 : o * 128 + MP] = hi * chosen[o]
            ml[o * 128 : o * 128 + MP] = lo * chosen[o]
        return fold(dot(bl[...], mh[...])) + dot(bl[0:MP], ml[...])

    def apply_both(it, block, coarse_copies, nb_copies):
        if it == 0:
            for copy in reb_copies:
                copy.wait_recv()
            partner_table()
            prepare_matrices()
            face_table(1, [nb[f : f + 1, :] for f in range(4)])
            for copy in nb_copies:
                copy.wait_recv()
            face_table(0, [nbg[0, f : f + 1, :] for f in range(4)])
            face_table(2, [nbg[1, f : f + 1, :] for f in range(4)])
        put_block(it, 0)
        for copy in coarse_copies:
            copy.wait_recv()
        coarse = coarse_solve(it)
        block[0].wait_recv()
        put_block(it, 1)
        theirs = gather(0, 2, 1)
        block[1].wait_recv()
        put_block(it, 2)
        block[2].wait_recv()
        put_block(it, 3)
        theirs = theirs + gather(2, 4, 1)
        give[it] = theirs[:MT]
        handed = start(remote(give.at[it], take.at[it], give_s.at[it], give_r.at[it], sib))
        mine = gather(0, 4, 0)
        handed.wait_recv()
        mixed = pad_rows(v[it] + F32(0.5) * (mine[:MT] + take[it]))
        keep = jnp.where(degree <= ords[...], F32(1.0), F32(0.0))
        z[it] = keep * smooth(mixed)[:MT]
        z[it, 0:2, :] = z[it, 0:2, :] + coarse[0:2]
        z[it, 10:12, :] = z[it, 10:12, :] + coarse[2:4]

        to_far = start(remote(z.at[it], halo.at[it, 1], halo_s.at[it, 1], halo_r.at[it, 1], line_dev(2 * c - 1)))
        to_near = start(remote(z.at[it], halo.at[it, 0], halo_s.at[it, 0], halo_r.at[it, 0], sib))

        hear(it)
        tell(it + 1)
        if it == 1:
            settle(len(pending) - 2)
        zv = pad_rows(z[it])
        hi, lo = split(zv)
        wl[0:MP, E : 2 * E] = hi
        wl[MP:, E : 2 * E] = lo
        kh[0:MP] = hi
        kl[0:MP] = lo
        own = fold(dot(sl[...], kh[...])) + dot(sl[0:MP], kl[...])
        base = scale[...] * own - F32(SHIFT) * zv
        nsum = fold(dot(wl[:, E : 2 * E], fsel[1, E : 2 * E, :]))
        outside = jnp.logical_or(
            jnp.logical_and(c == 0, line == 0), jnp.logical_and(c == 1, line == total - 1)
        )
        for side, copy in enumerate((to_near, to_far)):
            copy.wait_recv()
            field = halo[it, side]
            if side == 1:
                field = jnp.where(outside, F32(0.0), field)
            hi, lo = split(pad_rows(field))
            at = 2 * side * E
            wl[0:MP, at : at + E] = hi
            wl[MP:, at : at + E] = lo
            picked = pl.ds(pl.multiple_of(2 * E * (c if side == 1 else 1 - c), E), E)
            nsum = nsum + fold(dot(wl[:, at : at + E], fsel[1, picked, :]))
        hi, lo = split(nsum)
        kh[0:MP] = hi
        kl[0:MP] = lo
        faces = fold(dot(cl[...], kh[...])) + dot(cl[0:MP], kl[...])
        v[it + 1] = keep * (base - faces)[:MT]

    def gram(pairs):
        used = sorted({i for pair in pairs for i in pair})
        acc = {}
        for t in range(MT // 8):
            rows = {i: v[i, 8 * t : 8 * t + 8, :] for i in used}
            cut = {i: halves(rows[i]) for i in used}
            for a, b in pairs:
                prod, err = two_prod(rows[a], rows[b], cut[a], cut[b])
                if t == 0:
                    acc[a, b] = prod, err
                else:
                    s, e = two_sum(acc[a, b][0], prod)
                    acc[a, b] = s, acc[a, b][1] + (e + err)
        sums = []
        for pair in pairs:
            hi, lo = acc[pair]
            s, e = two_sum(hi[:, :128], hi[:, 128:])
            hi, lo = s, lo[:, :128] + lo[:, 128:] + e
            sums.append(roll_sum(hi, lo, 0, (4, 2, 1)))
        return sums

    def roll_sum(hi, lo, axis, shifts):
        for shift in shifts:
            s, e = two_sum(hi, pltpu.roll(hi, shift, axis))
            lo = lo + pltpu.roll(lo, shift, axis) + e
            hi = s
        return hi, lo

    reb_copies = [
        start(remote(rebg.at[pl.ds(0, 1)], rebg.at[pl.ds(o, 1)], reb_s.at[o - 1], reb_r.at[o - 1], group_dev(o)))
        for o in near
    ]
    coarse_copies = send_coarse(0)
    inputs[4].wait()
    nb_copies = [
        start(remote(nb, nbg.at[0], nb_s.at[0], nb_r.at[0], group_dev(1))),
        start(remote(nb, nbg.at[1], nb_s.at[1], nb_r.at[1], group_dev(-1))),
    ]
    block = send_block(0)
    tell(0)
    apply_both(0, block, coarse_copies, nb_copies)
    coarse_rows(1)
    sent = len(pending)
    coarse_copies = send_coarse(1)
    block = send_block(1)
    settle(sent)
    early = gram(((0, 0), (0, 1), (1, 1)))
    apply_both(1, block, coarse_copies, [])
    late = gram(((0, 2), (1, 2), (2, 2)))

    row, lane = iota((8, 128), 0), iota((8, 128), 1)

    def tree(x):
        err = None
        while x.shape[0] > 8:
            n = x.shape[0] // 2
            x, e = two_sum(x[:n], x[n:])
            err = e if err is None else err[:n] + err[n:] + e
        for shift in (4, 2, 1):
            x, e = two_sum(x, pltpu.roll(x, shift, 0))
            err = e if err is None else err + pltpu.roll(err, shift, 0) + e
        return x, err

    def carry(x, err):
        at = iota(x.shape, 1)
        return x + pltpu.roll(jnp.where(at < 8, err, F32(0.0)), 8, 1)

    hi = jnp.zeros((8, 128), F32)
    lo = jnp.zeros((8, 128), F32)
    for i, (h, l) in enumerate(early + late):
        hi = jnp.where(row == i, h, hi)
        lo = jnp.where(row == i, l, lo)
    rest = jnp.zeros((112, 128), F32)
    total_row = carry(*tree(jnp.concatenate([hi, lo, rest], axis=0).T))

    hear(2)
    def plane_hops(o):
        return min(o % 8, 8 - o % 8) // 2 + min(o // 8, n_y - o // 8)

    def z_hops(o):
        return min(o, n_z - o)

    base = 0
    for stage, (count, target, hops) in enumerate(((8 * n_y, plane_dev, plane_hops), (n_z, z_dev, z_hops))):
        rsrc[stage, 0:1, :] = total_row[0:1]
        sent = len(pending)
        copies = []
        for o in sorted(range(1, count), key=lambda o: -hops(o)):
            copies.append(
                start(
                    remote(
                        rsrc.at[stage, pl.ds(0, 1)],
                        red.at[stage, pl.ds(o, 1)],
                        red_s.at[base + o - 1],
                        red_r.at[base + o - 1],
                        target(o),
                    )
                )
            )
        red[stage, 0:1, :] = total_row[0:1]
        base += count - 1
        settle(sent)
        for copy in reversed(copies):
            copy.wait_recv()
        total_row = carry(*tree(red[stage]))

    def pick(i):
        return (pltpu.roll(total_row, 128 - i, 1) if i else total_row), pltpu.roll(total_row, 120 - i, 1)

    def less(a, factor, b):
        p, e = two_prod(factor, b[0])
        s, t = two_sum(a[0], -p)
        return s, (t - e) + (a[1] - factor * b[1])

    g01, g11, g02, g12, g22 = (pick(i) for i in range(1, 6))
    inverse = F32(1.0) / g11[0]
    q = g12[0] * inverse
    left_over = less(g12, q, g11)
    q_low = (left_over[0] + left_over[1]) * inverse
    top = less(g02, q, g01)
    bottom = less(g22, q, g12)
    beta = (top[0] + (top[1] - q_low * g01[0])) / (bottom[0] + (bottom[1] - q_low * g12[0]))
    rest = less(g01, beta, g12)
    alpha = (rest[0] + rest[1]) * inverse
    alpha, beta = alpha[0:1, 0:1], beta[0:1, 0:1]
    out[...] = alpha * z[0, 0:M, :] + beta * z[1, 0:M, :]
    for copy in pending:
        copy.wait_send()


def solution(mesh):
    n_wide = mesh.shape["wide"]
    n_z = 16 if n_wide == 64 else n_wide
    n_y = n_wide // n_z

    def per_device(right_side, orders, elem_scale, neighbours, rebalance, mode_diag, stiffness, coupling, block_inverse):
        hbm = pl.BlockSpec(memory_space=pltpu.HBM)
        dma = pltpu.SemaphoreType.DMA
        n_red = 8 * n_y - 1 + n_z - 1
        return pl.pallas_call(
            functools.partial(kernel, (n_wide, n_y, n_z)),
            out_shape=pltpu.VMEM((M, E), F32),
            in_specs=[hbm] * 9,
            out_specs=pl.BlockSpec(memory_space=pltpu.VMEM),
            scratch_shapes=[
                pltpu.VMEM((M, E), F32),
                pltpu.VMEM((1, E), jnp.int32),
                pltpu.VMEM((1, E), F32),
                pltpu.VMEM((4, E), jnp.int32),
                pltpu.VMEM((1, M), F32),
                pltpu.VMEM((M, M), F32),
                pltpu.VMEM((M, M), F32),
                pltpu.VMEM((ORDERS, M, M), F32),
                pltpu.VMEM((3, MT, E), F32),
                pltpu.VMEM((2, 3, MT, E), F32),
                pltpu.VMEM((2, MT, E), F32),
                pltpu.VMEM((2, 2, MT, E), F32),
                pltpu.VMEM((8, E), jnp.int32),
                pltpu.VMEM((8, E), jnp.int32),
                pltpu.VMEM((2, MT, E), F32),
                pltpu.VMEM((2, MT, E), F32),
                pltpu.VMEM((2, 5, 8, E), F32),
                pltpu.VMEM((2, 4, E), jnp.int32),
                pltpu.VMEM((2, 8, 128), F32),
                pltpu.VMEM((2, 32, 128), F32),
                pltpu.VMEM((9, MP, 128), F32),
                pltpu.VMEM((2, 8, 128), F32),
                pltpu.VMEM((2 * MP, ORDERS * 128), BF16),
                pltpu.VMEM((2 * MP, 128), BF16),
                pltpu.VMEM((2 * MP, 128), BF16),
                pltpu.VMEM((4 * E, 2 * E), BF16),
                pltpu.VMEM((3, 3 * E, E), BF16),
                pltpu.VMEM((2 * MP, 4 * E), BF16),
                pltpu.VMEM((2 * MP, 3 * E), BF16),
                pltpu.VMEM((ORDERS * 128, E), BF16),
                pltpu.VMEM((ORDERS * 128, E), BF16),
                pltpu.VMEM((128, E), BF16),
                pltpu.VMEM((128, E), BF16),
                pltpu.VMEM((ORDERS, MP, E), BF16),
                dma((9,)),
                dma((2, 3)),
                dma((2, 3)),
                dma,
                dma,
                dma((2,)),
                dma((2,)),
                dma((7,)),
                dma((7,)),
                dma((2, 4)),
                dma((2, 4)),
                dma((2,)),
                dma((2,)),
                dma((2, 2)),
                dma((2, 2)),
                dma((n_red,)),
                dma((n_red,)),
                pltpu.SemaphoreType.REGULAR((3,)),
            ],
            compiler_params=pltpu.CompilerParams(
                collective_id=0, has_side_effects=True, vmem_limit_bytes=60 * 1024 * 1024
            ),
        )(
            right_side,
            orders.reshape(1, E),
            elem_scale.reshape(1, E),
            neighbours,
            rebalance.reshape(1, E),
            mode_diag.reshape(1, M),
            stiffness,
            coupling,
            block_inverse,
        )

    line = ("wide", "narrow", "chip")
    return jax.shard_map(
        per_device,
        mesh=mesh,
        in_specs=(P(None, line), P(line), P(line), P(None, line), P(line), P(), P(), P(), P()),
        out_specs=P(None, line),
        check_vma=False,
    )
```

```python
import functools

import jax
import jax.numpy as jnp
from jax import lax
from jax.experimental import pallas as pl
from jax.experimental.pallas import tpu as pltpu
from jax.sharding import PartitionSpec as P

M = 100
MT = 104
MP = 112
E = 256
ORDERS = 6
MIN_ORDER = 4
SHIFT = 0.5
COARSE = (0, 1, 10, 11)
MESH = pl.DeviceIdType.MESH
F32 = jnp.float32
BF16 = jnp.bfloat16


def two_sum(a, b):
    s = a + b
    t = s - a
    return s, (a - (s - t)) + (b - t)


def halves(a):
    t = a * F32(4097.0)
    hi = t - (t - a)
    return hi, a - hi


def two_prod(a, b, a_parts=None, b_parts=None):
    ah, al = halves(a) if a_parts is None else a_parts
    bh, bl = halves(b) if b_parts is None else b_parts
    p = a * b
    return p, ((ah * bh - p) + ah * bl + al * bh) + al * bl


def split(x):
    hi = x.astype(BF16)
    return hi, (x - hi.astype(F32)).astype(BF16)


def dot(a, b):
    return jnp.dot(a, b, preferred_element_type=F32)


def iota(shape, axis):
    return lax.broadcasted_iota(jnp.int32, shape, axis)


def pad_rows(x):
    return jnp.concatenate([x, jnp.zeros((MP - MT, x.shape[1]), F32)], axis=0)


def fold(d):
    return d[:MP] + d[MP:]


def kernel(
    sizes,
    rs_h, ords_h, scale_h, nb_h, reb_h, diag_h, st_h, cp_h, bi_h, out,
    rs, ords, scale, reb, nb, diag, st, cp, bi,
    v, ag, z, halo, rebg, prow, give, take, cw, nbg, rsrc, red, pad, cpad,
    bl, sl, cl, tsel, fsel, gl, wl, mh, ml, kh, kl, chosen,
    in_s, sent_s, ag_r, pr_r, give_r, reb_r, cw_r, nb_r, halo_r, red_r, known,
):
    n_wide, n_y, n_z = sizes
    w, x, c = lax.axis_index("wide"), lax.axis_index("narrow"), lax.axis_index("chip")
    p = 2 * x + c
    line = w * 8 + p
    total = n_wide * 8
    wy, wz = lax.div(w, n_z), lax.rem(w, n_z)

    def group_dev(off):
        q = lax.rem(p + (off + 8), 8)
        return (w, lax.div(q, 2), lax.rem(q, 2))

    def line_dev(off):
        q = lax.rem(line + (off + total), total)
        return (lax.div(q, 8), lax.div(lax.rem(q, 8), 2), lax.rem(q, 2))

    def plane_dev(off):
        q = lax.rem(p + off % 8, 8)
        return (lax.rem(wy + off // 8, n_y) * n_z + wz, lax.div(q, 2), lax.rem(q, 2))

    def z_dev(off):
        return (wy * n_z + lax.rem(wz + (off + n_z), n_z), x, c)

    def both_ways(off):
        return [z_dev(off)] if 2 * off == n_z else [z_dev(off), z_dev(-off)]

    right, left = (w, lax.rem(x + 1, 4), c), (w, lax.rem(x + 3, 4), c)
    across, sib = (w, lax.rem(x + 2, 4), c), (w, x, 1 - c)

    inputs = [
        pltpu.make_async_copy(src, dst, in_s.at[i])
        for i, (src, dst) in enumerate(
            (
                (rs_h, rs), (ords_h, ords), (scale_h, scale), (reb_h, reb),
                (nb_h, nb), (diag_h, diag), (st_h, st), (cp_h, cp), (bi_h, bi),
            )
        )
    ]
    for copy in inputs[:4]:
        copy.start()

    barrier = pltpu.get_barrier_semaphore()
    near = (4, 3, 5, 2, 6, 1, 7)
    columns = [plane_dev(8 * o) for o in sorted(range(1, n_y), key=lambda o: -min(o, n_y - o))]
    greeted = columns + [line_dev(1), line_dev(-1)] + [group_dev(o) for o in near] + both_ways(1)
    for d in greeted:
        pl.semaphore_signal(barrier, inc=1, device_id=d, device_id_type=MESH)
    for copy in inputs[4:]:
        copy.start()

    rounds = [columns + both_ways(1)] + [both_ways(o) for o in (2, 4) if 2 * o < n_z]

    def tell(i):
        if i < len(rounds):
            for d in rounds[i]:
                pl.semaphore_signal(known.at[i], inc=1, device_id=d, device_id_type=MESH)

    def hear(i):
        if i < len(rounds):
            pl.semaphore_wait(known.at[i], len(rounds[i]))

    mode = iota((MT, E), 0)
    row_degree = (mode * 103) >> 10
    degree = jnp.maximum(row_degree, mode - 10 * row_degree)
    v[0, 96:MT, :] = jnp.zeros((8, E), F32)
    for copy in inputs[:4]:
        copy.wait()
    kept = jnp.where(degree <= ords[...], F32(1.0), F32(0.0))
    v[0, 0:M, :] = kept[0:M] * rs[...]
    for it in range(2):
        cw[it, 2] = jnp.zeros((8, E), F32)
        cw[it, 2, 4:5, :] = scale[...]

    def coarse_rows(it):
        cw[it, 2, 0:2, :] = v[it, 0:2, :]
        cw[it, 2, 2:4, :] = v[it, 10:12, :]

    coarse_rows(0)
    for stage, count in enumerate((8 * n_y, n_z)):
        if count < 32:
            red[stage, count:32, :] = jnp.zeros((32 - count, 128), F32)
    pl.semaphore_wait(barrier, len(greeted))

    slots = [0]

    def remote(src, dst, rsem, d):
        slots[0] += 1
        return pltpu.make_async_remote_copy(
            src_ref=src,
            dst_ref=dst,
            send_sem=sent_s.at[slots[0] - 1],
            recv_sem=rsem,
            device_id=d,
            device_id_type=MESH,
        )

    pending = []

    def start(copy):
        copy.start()
        pending.append(copy)
        return copy

    def settle(count):
        for copy in pending[:count]:
            copy.wait_send()
        del pending[:count]

    def send_coarse(it):
        copies = []
        for i, o in enumerate((1, -1, 2, -2)):
            copies.append(
                start(remote(cw.at[it, 2], cw.at[it, 2 - o], cw_r.at[it, i], group_dev(o)))
            )
        return copies

    def send_block(it):
        copies = [
            start(remote(v.at[it], ag.at[it, i], ag_r.at[it, i], d))
            for i, d in enumerate((across, right, left))
        ]
        return copies

    offsets = (0, 2, 3, 1)

    def put_block(it, b):
        hi, lo = split(pad_rows(v[it] if b == 0 else ag[it, b - 1]))
        gl[0:MP, b * E : (b + 1) * E] = hi
        gl[MP:, b * E : (b + 1) * E] = lo

    def gather(b0, b1, half):
        return fold(dot(gl[:, b0 * E : b1 * E], tsel[b0 * E : b1 * E, half * E : (half + 1) * E]))

    def prepare_matrices():
        for copy in inputs[5:]:
            copy.wait()
        pad[...] = jnp.zeros(pad.shape, F32)
        for o in range(ORDERS):
            pad[o, 0:M, 0:M] = bi[o]
        pad[6, 0:M, 0:M] = st[...]
        pad[7, 0:M, 0:M] = F32(0.25) * cp[...]
        pad[8, 0:1, 0:M] = diag[...]
        for o in range(ORDERS):
            hi, lo = split(pad[o])
            bl[0:MP, o * 128 : (o + 1) * 128] = hi
            bl[MP:, o * 128 : (o + 1) * 128] = lo
        s = pad[6]
        s = s + jnp.where(iota((MP, 128), 0) == iota((MP, 128), 1), pad[8, 0:1, :], F32(0.0))
        hi, lo = split(s)
        sl[0:MP] = hi
        sl[MP:] = lo
        pad[6] = s
        hi, lo = split(pad[7])
        cl[0:MP] = hi
        cl[MP:] = lo
        cpad[...] = jnp.zeros(cpad.shape, F32)
        for i in range(2):
            cpad[i, 0:2, :] = pad[6 + i, 0:2, :]
            cpad[i, 2:4, :] = pad[6 + i, 10:12, :]
        for ref in (kh, kl):
            ref[MP:128] = jnp.zeros((16, E), BF16)
        for o in range(ORDERS):
            chosen[o] = jnp.where(
                jnp.broadcast_to(ords[...], (MP, E)) == o + MIN_ORDER, F32(1.0), F32(0.0)
            ).astype(BF16)
            for ref in (mh, ml):
                ref[o * 128 + MP : (o + 1) * 128] = jnp.zeros((16, E), BF16)

    def partner_table():
        rows = rebg[...]
        even = iota((8, E), 1) % 2 == 0
        swapped = jnp.where(even, pltpu.roll(rows, E - 1, 1), pltpu.roll(rows, 1, 1)).astype(F32)
        me = iota((E, 128), 0) + p * E
        acc = jnp.zeros((E, 128), F32)
        for s in range(8):
            for h in range(2):
                lanes = slice(h * 128, (h + 1) * 128)
                acc = acc + jnp.where(rows[s : s + 1, lanes] == me, swapped[s : s + 1, lanes], F32(0.0))
        column = jnp.sum(acc, axis=1, keepdims=True)
        partner = jnp.sum(
            jnp.where(iota((E, E), 0) == iota((E, E), 1), column, F32(0.0)), axis=0, keepdims=True
        ).astype(jnp.int32)
        prow[0:1, :] = partner
        swap = start(remote(prow.at[pl.ds(0, 1)], prow.at[pl.ds(1, 1)], pr_r, sib))
        for half in range(2):
            if half == 1:
                swap.wait_recv()
            for b, r in enumerate(offsets):
                local = prow[half : half + 1, :] - (2 * lax.rem(x + r, 4) + c) * E

                @pl.loop(0, E // 64)
                def _(i):
                    hit = iota((64, E), 0) + i * 64 == local
                    tsel[pl.ds(b * E + i * 64, 64), half * E : (half + 1) * E] = jnp.where(
                        hit, F32(1.0), F32(0.0)
                    ).astype(BF16)

    def face_table(slot, index):
        @pl.loop(0, 3 * E // 64)
        def _(i):
            here = iota((64, E), 0) + i * 64
            count = jnp.zeros((64, E), F32)
            for f in range(4):
                count = count + jnp.where(here == index[f], F32(1.0), F32(0.0))
            fsel[slot, pl.ds(i * 64, 64), :] = count.astype(BF16)

    def coarse_solve(it):
        row = iota((8, E), 0)
        stiff = cpad[0]
        gain = cpad[1]
        s_col = [stiff[:, m : m + 1] for m in COARSE]
        g_col = [gain[:, m : m + 1] for m in COARSE]
        row1 = iota((8, 1), 0)
        dsum = jnp.zeros((8, 1), F32)
        for j in range(4):
            dsum = dsum + jnp.where(row1 == j, s_col[j], F32(0.0))
        rhs, scales, inverse, valid, y = [], [], [], [], []
        for o in range(-2, 3):
            ok = jnp.logical_and(p + o >= 0, p + o < 8)
            block = jnp.where(ok, cw[it, o + 2], F32(0.0))
            rhs.append(jnp.where(row < 4, block, F32(0.0)))
            scales.append(block[4:5])
            inverse.append(F32(1.0) / (block[4:5] * dsum - F32(SHIFT)))
            valid.append(ok)
            y.append(inverse[-1] * rhs[-1])

        def update(i, slot, y):
            window = jnp.concatenate([y[i - 1], y[i], y[i + 1]], axis=1)
            hi = window.astype(BF16).astype(F32)
            both = jnp.concatenate([hi, window - hi], axis=0).astype(BF16)
            d = dot(both, fsel[slot])
            nsum = d[0:8] + d[8:16]
            own = jnp.zeros((8, E), F32)
            faces = jnp.zeros((8, E), F32)
            for j in range(4):
                own = own + s_col[j] * y[i][j : j + 1]
                faces = faces + g_col[j] * nsum[j : j + 1]
            image = scales[i] * own - F32(SHIFT) * y[i] - faces
            new = y[i] + inverse[i] * (rhs[i] - image)
            return jnp.where(valid[i], new, F32(0.0))

        first = [None] + [update(i, i - 1, y) for i in (1, 2, 3)]
        return update(2, 1, first)

    def smooth(mixed):
        hi, lo = split(mixed)
        for o in range(ORDERS):
            mh[o * 128 : o * 128 + MP] = hi * chosen[o]
            ml[o * 128 : o * 128 + MP] = lo * chosen[o]
        return fold(dot(bl[...], mh[...])) + dot(bl[0:MP], ml[...])

    def apply_both(it, block, coarse_copies, nb_copies):
        if it == 0:
            pltpu.make_async_copy(rebg, rebg, reb_r).wait()
            partner_table()
            prepare_matrices()
            face_table(1, [nb[f : f + 1, :] for f in range(4)])
            for copy in nb_copies:
                copy.wait_recv()
            face_table(0, [nbg[0, f : f + 1, :] for f in range(4)])
            face_table(2, [nbg[1, f : f + 1, :] for f in range(4)])
        put_block(it, 0)
        for copy in coarse_copies:
            copy.wait_recv()
        coarse = coarse_solve(it)
        block[0].wait_recv()
        put_block(it, 1)
        theirs = gather(0, 2, 1)
        block[1].wait_recv()
        put_block(it, 2)
        block[2].wait_recv()
        put_block(it, 3)
        theirs = theirs + gather(2, 4, 1)
        give[it] = theirs[:MT]
        handed = start(remote(give.at[it], take.at[it], give_r.at[it], sib))
        mine = gather(0, 4, 0)
        handed.wait_recv()
        mixed = pad_rows(v[it] + F32(0.5) * (mine[:MT] + take[it]))
        keep = jnp.where(degree <= ords[...], F32(1.0), F32(0.0))
        z[it] = keep * smooth(mixed)[:MT]
        z[it, 0:2, :] = z[it, 0:2, :] + coarse[0:2]
        z[it, 10:12, :] = z[it, 10:12, :] + coarse[2:4]

        to_far = start(remote(z.at[it], halo.at[it, 1], halo_r.at[it, 1], line_dev(2 * c - 1)))
        to_near = start(remote(z.at[it], halo.at[it, 0], halo_r.at[it, 0], sib))

        hear(it)
        tell(it + 1)
        if it == 1:
            settle(len(pending) - 2)
        zv = pad_rows(z[it])
        hi, lo = split(zv)
        wl[0:MP, E : 2 * E] = hi
        wl[MP:, E : 2 * E] = lo
        kh[0:MP] = hi
        kl[0:MP] = lo
        own = fold(dot(sl[...], kh[...])) + dot(sl[0:MP], kl[...])
        base = scale[...] * own - F32(SHIFT) * zv
        nsum = fold(dot(wl[:, E : 2 * E], fsel[1, E : 2 * E, :]))
        outside = jnp.logical_or(
            jnp.logical_and(c == 0, line == 0), jnp.logical_and(c == 1, line == total - 1)
        )
        for side, copy in enumerate((to_near, to_far)):
            copy.wait_recv()
            field = halo[it, side]
            if side == 1:
                field = jnp.where(outside, F32(0.0), field)
            hi, lo = split(pad_rows(field))
            at = 2 * side * E
            wl[0:MP, at : at + E] = hi
            wl[MP:, at : at + E] = lo
            picked = pl.ds(pl.multiple_of(2 * E * (c if side == 1 else 1 - c), E), E)
            nsum = nsum + fold(dot(wl[:, at : at + E], fsel[1, picked, :]))
        hi, lo = split(nsum)
        kh[0:MP] = hi
        kl[0:MP] = lo
        faces = fold(dot(cl[...], kh[...])) + dot(cl[0:MP], kl[...])
        v[it + 1] = keep * (base - faces)[:MT]

    def gram(pairs):
        used = sorted({i for pair in pairs for i in pair})
        acc = {}
        for t in range(MT // 8):
            rows = {i: v[i, 8 * t : 8 * t + 8, :] for i in used}
            cut = {i: halves(rows[i]) for i in used}
            for a, b in pairs:
                prod, err = two_prod(rows[a], rows[b], cut[a], cut[b])
                if t == 0:
                    acc[a, b] = prod, err
                else:
                    s, e = two_sum(acc[a, b][0], prod)
                    acc[a, b] = s, acc[a, b][1] + (e + err)
        sums = []
        for pair in pairs:
            hi, lo = acc[pair]
            s, e = two_sum(hi[:, :128], hi[:, 128:])
            hi, lo = s, lo[:, :128] + lo[:, 128:] + e
            sums.append(roll_sum(hi, lo, 0, (4, 2, 1)))
        return sums

    def roll_sum(hi, lo, axis, shifts):
        for shift in shifts:
            s, e = two_sum(hi, pltpu.roll(hi, shift, axis))
            lo = lo + pltpu.roll(lo, shift, axis) + e
            hi = s
        return hi, lo

    for o in near:
        start(remote(reb, rebg.at[pl.ds(o, 1)], reb_r, group_dev(o)))
    pltpu.make_async_copy(reb, rebg.at[pl.ds(0, 1)], reb_r).start()
    coarse_copies = send_coarse(0)
    inputs[4].wait()
    nb_copies = [
        start(remote(nb, nbg.at[0], nb_r.at[0], group_dev(1))),
        start(remote(nb, nbg.at[1], nb_r.at[1], group_dev(-1))),
    ]
    block = send_block(0)
    tell(0)
    apply_both(0, block, coarse_copies, nb_copies)
    coarse_rows(1)
    sent = len(pending)
    coarse_copies = send_coarse(1)
    block = send_block(1)
    settle(sent)
    early = gram(((0, 0), (0, 1), (1, 1)))
    apply_both(1, block, coarse_copies, [])
    late = gram(((0, 2), (1, 2), (2, 2)))

    row, lane = iota((8, 128), 0), iota((8, 128), 1)

    def tree(x):
        err = None
        while x.shape[0] > 8:
            n = x.shape[0] // 2
            x, e = two_sum(x[:n], x[n:])
            err = e if err is None else err[:n] + err[n:] + e
        for shift in (4, 2, 1):
            x, e = two_sum(x, pltpu.roll(x, shift, 0))
            err = e if err is None else err + pltpu.roll(err, shift, 0) + e
        return x, err

    def carry(x, err):
        at = iota(x.shape, 1)
        return x + pltpu.roll(jnp.where(at < 8, err, F32(0.0)), 8, 1)

    hi = jnp.zeros((8, 128), F32)
    lo = jnp.zeros((8, 128), F32)
    for i, (h, l) in enumerate(early + late):
        hi = jnp.where(row == i, h, hi)
        lo = jnp.where(row == i, l, lo)
    rest = jnp.zeros((112, 128), F32)
    total_row = carry(*tree(jnp.concatenate([hi, lo, rest], axis=0).T))

    hear(2)
    def plane_hops(o):
        return min(o % 8, 8 - o % 8) // 2 + min(o // 8, n_y - o // 8)

    def z_hops(o):
        return min(o, n_z - o)

    settle(len(pending))
    slots[0] = 0
    for stage, (count, target, hops) in enumerate(((8 * n_y, plane_dev, plane_hops), (n_z, z_dev, z_hops))):
        rsrc[stage, 0:1, :] = total_row[0:1]
        sent = len(pending)
        source = rsrc.at[stage, pl.ds(0, 1)]
        for o in sorted(range(1, count), key=lambda o: -hops(o)):
            start(remote(source, red.at[stage, pl.ds(o, 1)], red_r.at[stage], target(o)))
        pltpu.make_async_copy(source, red.at[stage, pl.ds(0, 1)], red_r.at[stage]).start()
        settle(sent)
        all_rows = red.at[stage, pl.ds(0, count)]
        pltpu.make_async_copy(all_rows, all_rows, red_r.at[stage]).wait()
        total_row = carry(*tree(red[stage]))

    def pick(i):
        return (pltpu.roll(total_row, 128 - i, 1) if i else total_row), pltpu.roll(total_row, 120 - i, 1)

    def less(a, factor, b):
        p, e = two_prod(factor, b[0])
        s, t = two_sum(a[0], -p)
        return s, (t - e) + (a[1] - factor * b[1])

    g01, g11, g02, g12, g22 = (pick(i) for i in range(1, 6))
    inverse = F32(1.0) / g11[0]
    q = g12[0] * inverse
    left_over = less(g12, q, g11)
    q_low = (left_over[0] + left_over[1]) * inverse
    top = less(g02, q, g01)
    bottom = less(g22, q, g12)
    beta = (top[0] + (top[1] - q_low * g01[0])) / (bottom[0] + (bottom[1] - q_low * g12[0]))
    rest = less(g01, beta, g12)
    alpha = (rest[0] + rest[1]) * inverse
    alpha, beta = alpha[0:1, 0:1], beta[0:1, 0:1]
    out[...] = alpha * z[0, 0:M, :] + beta * z[1, 0:M, :]
    for copy in pending:
        copy.wait_send()


def solution(mesh):
    n_wide = mesh.shape["wide"]
    n_z = 16 if n_wide == 64 else n_wide
    n_y = n_wide // n_z

    def per_device(right_side, orders, elem_scale, neighbours, rebalance, mode_diag, stiffness, coupling, block_inverse):
        hbm = pl.BlockSpec(memory_space=pltpu.HBM)
        dma = pltpu.SemaphoreType.DMA
        n_red = 8 * n_y - 1 + n_z - 1
        return pl.pallas_call(
            functools.partial(kernel, (n_wide, n_y, n_z)),
            out_shape=pltpu.VMEM((M, E), F32),
            in_specs=[hbm] * 9,
            out_specs=pl.BlockSpec(memory_space=pltpu.VMEM),
            scratch_shapes=[
                pltpu.VMEM((M, E), F32),
                pltpu.VMEM((1, E), jnp.int32),
                pltpu.VMEM((1, E), F32),
                pltpu.VMEM((1, E), jnp.int32),
                pltpu.VMEM((4, E), jnp.int32),
                pltpu.VMEM((1, M), F32),
                pltpu.VMEM((M, M), F32),
                pltpu.VMEM((M, M), F32),
                pltpu.VMEM((ORDERS, M, M), F32),
                pltpu.VMEM((3, MT, E), F32),
                pltpu.VMEM((2, 3, MT, E), F32),
                pltpu.VMEM((2, MT, E), F32),
                pltpu.VMEM((2, 2, MT, E), F32),
                pltpu.VMEM((8, E), jnp.int32),
                pltpu.VMEM((8, E), jnp.int32),
                pltpu.VMEM((2, MT, E), F32),
                pltpu.VMEM((2, MT, E), F32),
                pltpu.VMEM((2, 5, 8, E), F32),
                pltpu.VMEM((2, 4, E), jnp.int32),
                pltpu.VMEM((2, 8, 128), F32),
                pltpu.VMEM((2, 32, 128), F32),
                pltpu.VMEM((9, MP, 128), F32),
                pltpu.VMEM((2, 8, 128), F32),
                pltpu.VMEM((2 * MP, ORDERS * 128), BF16),
                pltpu.VMEM((2 * MP, 128), BF16),
                pltpu.VMEM((2 * MP, 128), BF16),
                pltpu.VMEM((4 * E, 2 * E), BF16),
                pltpu.VMEM((3, 3 * E, E), BF16),
                pltpu.VMEM((2 * MP, 4 * E), BF16),
                pltpu.VMEM((2 * MP, 3 * E), BF16),
                pltpu.VMEM((ORDERS * 128, E), BF16),
                pltpu.VMEM((ORDERS * 128, E), BF16),
                pltpu.VMEM((128, E), BF16),
                pltpu.VMEM((128, E), BF16),
                pltpu.VMEM((ORDERS, MP, E), BF16),
                dma((9,)),
                dma((max(n_red, 31),)),
                dma((2, 3)),
                dma,
                dma((2,)),
                dma,
                dma((2, 4)),
                dma((2,)),
                dma((2, 2)),
                dma((2,)),
                pltpu.SemaphoreType.REGULAR((3,)),
            ],
            compiler_params=pltpu.CompilerParams(
                collective_id=0, has_side_effects=True, vmem_limit_bytes=60 * 1024 * 1024
            ),
        )(
            right_side,
            orders.reshape(1, E),
            elem_scale.reshape(1, E),
            neighbours,
            rebalance.reshape(1, E),
            mode_diag.reshape(1, M),
            stiffness,
            coupling,
            block_inverse,
        )

    line = ("wide", "narrow", "chip")
    return jax.shard_map(
        per_device,
        mesh=mesh,
        in_specs=(P(None, line), P(line), P(line), P(None, line), P(line), P(), P(), P(), P()),
        out_specs=P(None, line),
        check_vma=False,
    )
```

```python
import functools

import jax
import jax.numpy as jnp
from jax import lax
from jax.experimental import pallas as pl
from jax.experimental.pallas import tpu as pltpu
from jax.sharding import PartitionSpec as P

M = 100
MT = 104
MP = 112
E = 256
ORDERS = 6
MIN_ORDER = 4
SHIFT = 0.5
COARSE = (0, 1, 10, 11)
MESH = pl.DeviceIdType.MESH
F32 = jnp.float32
BF16 = jnp.bfloat16


def two_sum(a, b):
    s = a + b
    t = s - a
    return s, (a - (s - t)) + (b - t)


def halves(a):
    t = a * F32(4097.0)
    hi = t - (t - a)
    return hi, a - hi


def two_prod(a, b, a_parts=None, b_parts=None):
    ah, al = halves(a) if a_parts is None else a_parts
    bh, bl = halves(b) if b_parts is None else b_parts
    p = a * b
    return p, ((ah * bh - p) + ah * bl + al * bh) + al * bl


def split(x):
    hi = x.astype(BF16)
    return hi, (x - hi.astype(F32)).astype(BF16)


def dot(a, b):
    return jnp.dot(a, b, preferred_element_type=F32)


def iota(shape, axis):
    return lax.broadcasted_iota(jnp.int32, shape, axis)


def pad_rows(x):
    return jnp.concatenate([x, jnp.zeros((MP - MT, x.shape[1]), F32)], axis=0)


def fold(d):
    return d[:MP] + d[MP:]


def kernel(
    sizes,
    rs_h, ords_h, scale_h, nb_h, reb_h, diag_h, st_h, cp_h, bi_h, out,
    rs, ords, scale, reb, nb, diag, st, cp, bi,
    v, ag, z, halo, rebg, prow, give, take, cw, nbg, rsrc, red, spare, pad, cpad,
    bl, sl, cl, tsel, fsel, gl, wl, mh, ml, kh, kl, chosen,
    in_s, sent_s, ag_r, pr_r, give_r, reb_r, cw_r, nb_r, halo_r, red_r, red_s, known,
):
    n_wide, n_y, n_z = sizes
    w, x, c = lax.axis_index("wide"), lax.axis_index("narrow"), lax.axis_index("chip")
    p = 2 * x + c
    line = w * 8 + p
    total = n_wide * 8
    wy, wz = lax.div(w, n_z), lax.rem(w, n_z)

    def group_dev(off):
        q = lax.rem(p + (off + 8), 8)
        return (w, lax.div(q, 2), lax.rem(q, 2))

    def line_dev(off):
        q = lax.rem(line + (off + total), total)
        return (lax.div(q, 8), lax.div(lax.rem(q, 8), 2), lax.rem(q, 2))

    def plane_dev(off):
        q = lax.rem(p + off % 8, 8)
        return (lax.rem(wy + off // 8, n_y) * n_z + wz, lax.div(q, 2), lax.rem(q, 2))

    def z_dev(off):
        return (wy * n_z + lax.rem(wz + (off + n_z), n_z), x, c)

    def both_ways(off):
        return [z_dev(off)] if 2 * off == n_z else [z_dev(off), z_dev(-off)]

    right, left = (w, lax.rem(x + 1, 4), c), (w, lax.rem(x + 3, 4), c)
    across, sib = (w, lax.rem(x + 2, 4), c), (w, x, 1 - c)

    inputs = [
        pltpu.make_async_copy(src, dst, in_s.at[i])
        for i, (src, dst) in enumerate(
            (
                (rs_h, rs), (ords_h, ords), (scale_h, scale), (reb_h, reb),
                (nb_h, nb), (diag_h, diag), (st_h, st), (cp_h, cp), (bi_h, bi),
            )
        )
    ]
    for copy in inputs[:4]:
        copy.start()

    barrier = pltpu.get_barrier_semaphore()
    near = (4, 3, 5, 2, 6, 1, 7)
    columns = [plane_dev(8 * o) for o in sorted(range(1, n_y), key=lambda o: -min(o, n_y - o))]
    greeted = columns + [line_dev(1), line_dev(-1)] + [group_dev(o) for o in near] + both_ways(1)
    for d in greeted:
        pl.semaphore_signal(barrier, inc=1, device_id=d, device_id_type=MESH)
    for copy in inputs[4:]:
        copy.start()

    rounds = [columns + both_ways(1)] + [both_ways(o) for o in (2, 4) if 2 * o < n_z]

    def tell(i):
        if i < len(rounds):
            for d in rounds[i]:
                pl.semaphore_signal(known.at[i], inc=1, device_id=d, device_id_type=MESH)

    def hear(i):
        if i < len(rounds):
            pl.semaphore_wait(known.at[i], len(rounds[i]))

    mode = iota((MT, E), 0)
    row_degree = (mode * 103) >> 10
    degree = jnp.maximum(row_degree, mode - 10 * row_degree)
    v[0, 96:MT, :] = jnp.zeros((8, E), F32)
    for copy in inputs[:4]:
        copy.wait()
    kept = jnp.where(degree <= ords[...], F32(1.0), F32(0.0))
    v[0, 0:M, :] = kept[0:M] * rs[...]
    for it in range(2):
        cw[it, 2] = jnp.zeros((8, E), F32)
        cw[it, 2, 4:5, :] = scale[...]

    def coarse_rows(it):
        cw[it, 2, 0:2, :] = v[it, 0:2, :]
        cw[it, 2, 2:4, :] = v[it, 10:12, :]

    coarse_rows(0)
    for stage, count in enumerate((8 * n_y, n_z)):
        if count < 32:
            red[stage, count:32, :] = jnp.zeros((32 - count, 128), F32)
    pl.semaphore_wait(barrier, len(greeted))

    slots = [0]

    def remote(src, dst, rsem, d, ssem=None):
        if ssem is None:
            ssem = sent_s.at[slots[0]]
            slots[0] += 1
        return pltpu.make_async_remote_copy(
            src_ref=src,
            dst_ref=dst,
            send_sem=ssem,
            recv_sem=rsem,
            device_id=d,
            device_id_type=MESH,
        )

    pending = []

    def start(copy):
        copy.start()
        pending.append(copy)
        return copy

    def settle(count):
        for copy in pending[:count]:
            copy.wait_send()
        del pending[:count]

    def send_coarse(it):
        copies = []
        for i, o in enumerate((1, -1, 2, -2)):
            copies.append(
                start(remote(cw.at[it, 2], cw.at[it, 2 - o], cw_r.at[it, i], group_dev(o)))
            )
        return copies

    def send_block(it):
        copies = [
            start(remote(v.at[it], ag.at[it, i], ag_r.at[it, i], d))
            for i, d in enumerate((across, right, left))
        ]
        return copies

    offsets = (0, 2, 3, 1)

    def put_block(it, b):
        hi, lo = split(pad_rows(v[it] if b == 0 else ag[it, b - 1]))
        gl[0:MP, b * E : (b + 1) * E] = hi
        gl[MP:, b * E : (b + 1) * E] = lo

    def gather(b0, b1, half):
        return fold(dot(gl[:, b0 * E : b1 * E], tsel[b0 * E : b1 * E, half * E : (half + 1) * E]))

    def prepare_matrices():
        for copy in inputs[5:]:
            copy.wait()
        pad[...] = jnp.zeros(pad.shape, F32)
        for o in range(ORDERS):
            pad[o, 0:M, 0:M] = bi[o]
        pad[6, 0:M, 0:M] = st[...]
        pad[7, 0:M, 0:M] = F32(0.25) * cp[...]
        pad[8, 0:1, 0:M] = diag[...]
        for o in range(ORDERS):
            hi, lo = split(pad[o])
            bl[0:MP, o * 128 : (o + 1) * 128] = hi
            bl[MP:, o * 128 : (o + 1) * 128] = lo
        s = pad[6]
        s = s + jnp.where(iota((MP, 128), 0) == iota((MP, 128), 1), pad[8, 0:1, :], F32(0.0))
        hi, lo = split(s)
        sl[0:MP] = hi
        sl[MP:] = lo
        pad[6] = s
        hi, lo = split(pad[7])
        cl[0:MP] = hi
        cl[MP:] = lo
        cpad[...] = jnp.zeros(cpad.shape, F32)
        for i in range(2):
            cpad[i, 0:2, :] = pad[6 + i, 0:2, :]
            cpad[i, 2:4, :] = pad[6 + i, 10:12, :]
        for ref in (kh, kl):
            ref[MP:128] = jnp.zeros((16, E), BF16)
        for o in range(ORDERS):
            chosen[o] = jnp.where(
                jnp.broadcast_to(ords[...], (MP, E)) == o + MIN_ORDER, F32(1.0), F32(0.0)
            ).astype(BF16)
            for ref in (mh, ml):
                ref[o * 128 + MP : (o + 1) * 128] = jnp.zeros((16, E), BF16)

    def partner_table():
        rows = rebg[...]
        even = iota((8, E), 1) % 2 == 0
        swapped = jnp.where(even, pltpu.roll(rows, E - 1, 1), pltpu.roll(rows, 1, 1)).astype(F32)
        me = iota((E, 128), 0) + p * E
        acc = jnp.zeros((E, 128), F32)
        for s in range(8):
            for h in range(2):
                lanes = slice(h * 128, (h + 1) * 128)
                acc = acc + jnp.where(rows[s : s + 1, lanes] == me, swapped[s : s + 1, lanes], F32(0.0))
        column = jnp.sum(acc, axis=1, keepdims=True)
        partner = jnp.sum(
            jnp.where(iota((E, E), 0) == iota((E, E), 1), column, F32(0.0)), axis=0, keepdims=True
        ).astype(jnp.int32)
        prow[0:1, :] = partner
        swap = start(remote(prow.at[pl.ds(0, 1)], prow.at[pl.ds(1, 1)], pr_r, sib))
        for half in range(2):
            if half == 1:
                swap.wait_recv()
            for b, r in enumerate(offsets):
                local = prow[half : half + 1, :] - (2 * lax.rem(x + r, 4) + c) * E

                @pl.loop(0, E // 64)
                def _(i):
                    hit = iota((64, E), 0) + i * 64 == local
                    tsel[pl.ds(b * E + i * 64, 64), half * E : (half + 1) * E] = jnp.where(
                        hit, F32(1.0), F32(0.0)
                    ).astype(BF16)

    def face_table(slot, index):
        @pl.loop(0, 3 * E // 64)
        def _(i):
            here = iota((64, E), 0) + i * 64
            count = jnp.zeros((64, E), F32)
            for f in range(4):
                count = count + jnp.where(here == index[f], F32(1.0), F32(0.0))
            fsel[slot, pl.ds(i * 64, 64), :] = count.astype(BF16)

    def coarse_solve(it):
        row = iota((8, E), 0)
        stiff = cpad[0]
        gain = cpad[1]
        s_col = [stiff[:, m : m + 1] for m in COARSE]
        g_col = [gain[:, m : m + 1] for m in COARSE]
        row1 = iota((8, 1), 0)
        dsum = jnp.zeros((8, 1), F32)
        for j in range(4):
            dsum = dsum + jnp.where(row1 == j, s_col[j], F32(0.0))
        rhs, scales, inverse, valid, y = [], [], [], [], []
        for o in range(-2, 3):
            ok = jnp.logical_and(p + o >= 0, p + o < 8)
            block = jnp.where(ok, cw[it, o + 2], F32(0.0))
            rhs.append(jnp.where(row < 4, block, F32(0.0)))
            scales.append(block[4:5])
            inverse.append(F32(1.0) / (block[4:5] * dsum - F32(SHIFT)))
            valid.append(ok)
            y.append(inverse[-1] * rhs[-1])

        def update(i, slot, y):
            window = jnp.concatenate([y[i - 1], y[i], y[i + 1]], axis=1)
            hi = window.astype(BF16).astype(F32)
            both = jnp.concatenate([hi, window - hi], axis=0).astype(BF16)
            d = dot(both, fsel[slot])
            nsum = d[0:8] + d[8:16]
            own = jnp.zeros((8, E), F32)
            faces = jnp.zeros((8, E), F32)
            for j in range(4):
                own = own + s_col[j] * y[i][j : j + 1]
                faces = faces + g_col[j] * nsum[j : j + 1]
            image = scales[i] * own - F32(SHIFT) * y[i] - faces
            new = y[i] + inverse[i] * (rhs[i] - image)
            return jnp.where(valid[i], new, F32(0.0))

        first = [None] + [update(i, i - 1, y) for i in (1, 2, 3)]
        return update(2, 1, first)

    def smooth(mixed):
        hi, lo = split(mixed)
        for o in range(ORDERS):
            mh[o * 128 : o * 128 + MP] = hi * chosen[o]
            ml[o * 128 : o * 128 + MP] = lo * chosen[o]
        return fold(dot(bl[...], mh[...])) + dot(bl[0:MP], ml[...])

    def apply_both(it, block, coarse_copies, nb_copies):
        if it == 0:
            pltpu.make_async_copy(rebg, rebg, reb_r).wait()
            partner_table()
            prepare_matrices()
            face_table(1, [nb[f : f + 1, :] for f in range(4)])
            for copy in nb_copies:
                copy.wait_recv()
            face_table(0, [nbg[0, f : f + 1, :] for f in range(4)])
            face_table(2, [nbg[1, f : f + 1, :] for f in range(4)])
        put_block(it, 0)
        for copy in coarse_copies:
            copy.wait_recv()
        coarse = coarse_solve(it)
        block[0].wait_recv()
        put_block(it, 1)
        theirs = gather(0, 2, 1)
        block[1].wait_recv()
        put_block(it, 2)
        block[2].wait_recv()
        put_block(it, 3)
        theirs = theirs + gather(2, 4, 1)
        give[it] = theirs[:MT]
        handed = start(remote(give.at[it], take.at[it], give_r.at[it], sib))
        mine = gather(0, 4, 0)
        handed.wait_recv()
        mixed = pad_rows(v[it] + F32(0.5) * (mine[:MT] + take[it]))
        keep = jnp.where(degree <= ords[...], F32(1.0), F32(0.0))
        z[it] = keep * smooth(mixed)[:MT]
        z[it, 0:2, :] = z[it, 0:2, :] + coarse[0:2]
        z[it, 10:12, :] = z[it, 10:12, :] + coarse[2:4]

        to_far = start(remote(z.at[it], halo.at[it, 1], halo_r.at[it, 1], line_dev(2 * c - 1)))
        to_near = start(remote(z.at[it], halo.at[it, 0], halo_r.at[it, 0], sib))

        hear(it)
        tell(it + 1)
        if it == 1:
            settle(len(pending) - 2)
        zv = pad_rows(z[it])
        hi, lo = split(zv)
        wl[0:MP, E : 2 * E] = hi
        wl[MP:, E : 2 * E] = lo
        kh[0:MP] = hi
        kl[0:MP] = lo
        own = fold(dot(sl[...], kh[...])) + dot(sl[0:MP], kl[...])
        base = scale[...] * own - F32(SHIFT) * zv
        nsum = fold(dot(wl[:, E : 2 * E], fsel[1, E : 2 * E, :]))
        outside = jnp.logical_or(
            jnp.logical_and(c == 0, line == 0), jnp.logical_and(c == 1, line == total - 1)
        )
        for side, copy in enumerate((to_near, to_far)):
            copy.wait_recv()
            field = halo[it, side]
            if side == 1:
                field = jnp.where(outside, F32(0.0), field)
            hi, lo = split(pad_rows(field))
            at = 2 * side * E
            wl[0:MP, at : at + E] = hi
            wl[MP:, at : at + E] = lo
            picked = pl.ds(pl.multiple_of(2 * E * (c if side == 1 else 1 - c), E), E)
            nsum = nsum + fold(dot(wl[:, at : at + E], fsel[1, picked, :]))
        hi, lo = split(nsum)
        kh[0:MP] = hi
        kl[0:MP] = lo
        faces = fold(dot(cl[...], kh[...])) + dot(cl[0:MP], kl[...])
        v[it + 1] = keep * (base - faces)[:MT]

    def gram(pairs):
        used = sorted({i for pair in pairs for i in pair})
        acc = {}
        for t in range(MT // 8):
            rows = {i: v[i, 8 * t : 8 * t + 8, :] for i in used}
            cut = {i: halves(rows[i]) for i in used}
            for a, b in pairs:
                prod, err = two_prod(rows[a], rows[b], cut[a], cut[b])
                if t == 0:
                    acc[a, b] = prod, err
                else:
                    s, e = two_sum(acc[a, b][0], prod)
                    acc[a, b] = s, acc[a, b][1] + (e + err)
        sums = []
        for pair in pairs:
            hi, lo = acc[pair]
            s, e = two_sum(hi[:, :128], hi[:, 128:])
            hi, lo = s, lo[:, :128] + lo[:, 128:] + e
            sums.append(roll_sum(hi, lo, 0, (4, 2, 1)))
        return sums

    def roll_sum(hi, lo, axis, shifts):
        for shift in shifts:
            s, e = two_sum(hi, pltpu.roll(hi, shift, axis))
            lo = lo + pltpu.roll(lo, shift, axis) + e
            hi = s
        return hi, lo

    for o in near:
        start(remote(reb, rebg.at[pl.ds(o, 1)], reb_r, group_dev(o)))
    pltpu.make_async_copy(reb, rebg.at[pl.ds(0, 1)], reb_r).start()
    coarse_copies = send_coarse(0)
    inputs[4].wait()
    nb_copies = [
        start(remote(nb, nbg.at[0], nb_r.at[0], group_dev(1))),
        start(remote(nb, nbg.at[1], nb_r.at[1], group_dev(-1))),
    ]
    block = send_block(0)
    tell(0)
    apply_both(0, block, coarse_copies, nb_copies)
    coarse_rows(1)
    sent = len(pending)
    coarse_copies = send_coarse(1)
    block = send_block(1)
    settle(sent)
    early = gram(((0, 0), (0, 1), (1, 1)))
    apply_both(1, block, coarse_copies, [])
    late = gram(((0, 2), (1, 2), (2, 2)))

    row, lane = iota((8, 128), 0), iota((8, 128), 1)

    def tree(x):
        err = None
        while x.shape[0] > 8:
            n = x.shape[0] // 2
            x, e = two_sum(x[:n], x[n:])
            err = e if err is None else err[:n] + err[n:] + e
        for shift in (4, 2, 1):
            x, e = two_sum(x, pltpu.roll(x, shift, 0))
            err = e if err is None else err + pltpu.roll(err, shift, 0) + e
        return x, err

    def carry(x, err):
        at = iota(x.shape, 1)
        return x + pltpu.roll(jnp.where(at < 8, err, F32(0.0)), 8, 1)

    hi = jnp.zeros((8, 128), F32)
    lo = jnp.zeros((8, 128), F32)
    for i, (h, l) in enumerate(early + late):
        hi = jnp.where(row == i, h, hi)
        lo = jnp.where(row == i, l, lo)
    rest = jnp.zeros((112, 128), F32)
    total_row = carry(*tree(jnp.concatenate([hi, lo, rest], axis=0).T))

    hear(2)
    def plane_hops(o):
        return min(o % 8, 8 - o % 8) // 2 + min(o // 8, n_y - o // 8)

    def z_hops(o):
        return min(o, n_z - o)

    settle(len(pending))
    for stage, (count, target, hops) in enumerate(((8 * n_y, plane_dev, plane_hops), (n_z, z_dev, z_hops))):
        rsrc[stage, 0:1, :] = total_row[0:1]
        source = rsrc.at[stage, pl.ds(0, 1)]
        for o in sorted(range(1, count), key=lambda o: -hops(o)):
            remote(
                source, red.at[stage, pl.ds(o, 1)], red_r.at[stage], target(o), red_s.at[stage]
            ).start()
        pltpu.make_async_copy(source, red.at[stage, pl.ds(0, 1)], red_r.at[stage]).start()
        pltpu.make_async_copy(source, spare.at[stage, pl.ds(0, 1)], red_s.at[stage]).start()
        all_rows = red.at[stage, pl.ds(0, count)]
        pltpu.make_async_copy(all_rows, all_rows, red_r.at[stage]).wait()
        pltpu.make_async_copy(all_rows, all_rows, red_s.at[stage]).wait()
        total_row = carry(*tree(red[stage]))

    def pick(i):
        return (pltpu.roll(total_row, 128 - i, 1) if i else total_row), pltpu.roll(total_row, 120 - i, 1)

    def less(a, factor, b):
        p, e = two_prod(factor, b[0])
        s, t = two_sum(a[0], -p)
        return s, (t - e) + (a[1] - factor * b[1])

    g01, g11, g02, g12, g22 = (pick(i) for i in range(1, 6))
    inverse = F32(1.0) / g11[0]
    q = g12[0] * inverse
    left_over = less(g12, q, g11)
    q_low = (left_over[0] + left_over[1]) * inverse
    top = less(g02, q, g01)
    bottom = less(g22, q, g12)
    beta = (top[0] + (top[1] - q_low * g01[0])) / (bottom[0] + (bottom[1] - q_low * g12[0]))
    rest = less(g01, beta, g12)
    alpha = (rest[0] + rest[1]) * inverse
    alpha, beta = alpha[0:1, 0:1], beta[0:1, 0:1]
    out[...] = alpha * z[0, 0:M, :] + beta * z[1, 0:M, :]
    for copy in pending:
        copy.wait_send()


def solution(mesh):
    n_wide = mesh.shape["wide"]
    n_z = 16 if n_wide == 64 else n_wide
    n_y = n_wide // n_z

    def per_device(right_side, orders, elem_scale, neighbours, rebalance, mode_diag, stiffness, coupling, block_inverse):
        hbm = pl.BlockSpec(memory_space=pltpu.HBM)
        dma = pltpu.SemaphoreType.DMA
        return pl.pallas_call(
            functools.partial(kernel, (n_wide, n_y, n_z)),
            out_shape=pltpu.VMEM((M, E), F32),
            in_specs=[hbm] * 9,
            out_specs=pl.BlockSpec(memory_space=pltpu.VMEM),
            scratch_shapes=[
                pltpu.VMEM((M, E), F32),
                pltpu.VMEM((1, E), jnp.int32),
                pltpu.VMEM((1, E), F32),
                pltpu.VMEM((1, E), jnp.int32),
                pltpu.VMEM((4, E), jnp.int32),
                pltpu.VMEM((1, M), F32),
                pltpu.VMEM((M, M), F32),
                pltpu.VMEM((M, M), F32),
                pltpu.VMEM((ORDERS, M, M), F32),
                pltpu.VMEM((3, MT, E), F32),
                pltpu.VMEM((2, 3, MT, E), F32),
                pltpu.VMEM((2, MT, E), F32),
                pltpu.VMEM((2, 2, MT, E), F32),
                pltpu.VMEM((8, E), jnp.int32),
                pltpu.VMEM((8, E), jnp.int32),
                pltpu.VMEM((2, MT, E), F32),
                pltpu.VMEM((2, MT, E), F32),
                pltpu.VMEM((2, 5, 8, E), F32),
                pltpu.VMEM((2, 4, E), jnp.int32),
                pltpu.VMEM((2, 8, 128), F32),
                pltpu.VMEM((2, 32, 128), F32),
                pltpu.VMEM((2, 8, 128), F32),
                pltpu.VMEM((9, MP, 128), F32),
                pltpu.VMEM((2, 8, 128), F32),
                pltpu.VMEM((2 * MP, ORDERS * 128), BF16),
                pltpu.VMEM((2 * MP, 128), BF16),
                pltpu.VMEM((2 * MP, 128), BF16),
                pltpu.VMEM((4 * E, 2 * E), BF16),
                pltpu.VMEM((3, 3 * E, E), BF16),
                pltpu.VMEM((2 * MP, 4 * E), BF16),
                pltpu.VMEM((2 * MP, 3 * E), BF16),
                pltpu.VMEM((ORDERS * 128, E), BF16),
                pltpu.VMEM((ORDERS * 128, E), BF16),
                pltpu.VMEM((128, E), BF16),
                pltpu.VMEM((128, E), BF16),
                pltpu.VMEM((ORDERS, MP, E), BF16),
                dma((9,)),
                dma((30,)),
                dma((2, 3)),
                dma,
                dma((2,)),
                dma,
                dma((2, 4)),
                dma((2,)),
                dma((2, 2)),
                dma((2,)),
                dma((2,)),
                pltpu.SemaphoreType.REGULAR((3,)),
            ],
            compiler_params=pltpu.CompilerParams(
                collective_id=0, has_side_effects=True, vmem_limit_bytes=60 * 1024 * 1024
            ),
        )(
            right_side,
            orders.reshape(1, E),
            elem_scale.reshape(1, E),
            neighbours,
            rebalance.reshape(1, E),
            mode_diag.reshape(1, M),
            stiffness,
            coupling,
            block_inverse,
        )

    line = ("wide", "narrow", "chip")
    return jax.shard_map(
        per_device,
        mesh=mesh,
        in_specs=(P(None, line), P(line), P(line), P(None, line), P(line), P(), P(), P(), P()),
        out_specs=P(None, line),
        check_vma=False,
    )
```
